512 devices in a mesh: ctx: 128 (over y, x, z_lo), head: 4 (over z_hi, core).
Axes of the slice: x: 4, y: 8, z: 8 (z_hi: 2, z_lo: 4; z = z_hi * 4 + z_lo), core: 2. Of those that a mesh axis runs over, the one named last changes fastest.
Arguments:
- q_nope: bfloat16 [16384, 8192], P('ctx', 'head'), may hold values from -480 to 480
- q_rope: bfloat16 [16384, 4096], P('ctx', 'head'), may hold values from -6 to 6
- latent: bfloat16 [16384, 512], P('ctx'), may hold values from -6 to 6
- key_rope: bfloat16 [16384, 64], P('ctx'), may hold values from -6 to 6
- w_key: bfloat16 [512, 8192], P('ctx', 'head'), may hold values from -0.25 to 0.25
- w_value: bfloat16 [512, 8192], P('ctx', 'head'), may hold values from -0.25 to 0.25
- stripe: int32 [16384], replicated, may hold values from 0 to 16383, as said below
- frame_len: int32 [129], replicated, may hold values from 1 to 254, as said below
- out_grad: bfloat16 [16384, 8192], P('ctx', 'head'), may hold values from -6 to 6
Outputs:
- attended: bfloat16 [16384, 8192], P('ctx', 'head')
- dq_nope: float32 [16384, 8192], P('ctx', 'head')
- dq_rope: float32 [16384, 4096], P('ctx', 'head')
- d_latent: float32 [16384, 512], P('ctx')
- d_key_rope: float32 [16384, 64], P('ctx')
The draws below stay inside these ranges and needn't reach their ends.
Inputs may be any that keep to these rules, and one draw needn't show every extreme that they name: `stripe`: rows c * 128 to (c + 1) * 128 - 1 hold the episode positions c * 128 to (c + 1) * 128 - 1 in some order, each once. `frame_len`: frame 0 starts at position 0; every later frame k starts at (k - 1) * 128 + u with 1 <= u <= 127; the lengths sum to 16384.
All inputs are finite; a program needn't handle non-finite values.
Results may differ from the reference program's by a relative error of at most 0.028.
The reference program's roundings to bfloat16 on the way (of `keys`, `values`, `probs`, `score_grad`, `key_part` and `value_part`) count: a program that leaves them out, or rounds other values in their place, can miss the bound.
Values may be sent and summed in bfloat16 or wider, within the bound.
A program may use at most 64 MiB of HBM per device.

```python
import jax
import jax.numpy as jnp
from jax import lax

HEADS = 64
HEAD_DIM = 128
LATENT = 512
ROPE = 64
HEAD_QK = 192
WINDOW = 128
TOK_DEV = 128
TOKENS = 16384


def draw_q_nope(key, part):
    key = jax.random.fold_in(key, 5)
    first_key = jax.random.fold_in(key, 0)
    values = jax.random.truncated_normal(first_key, -6.0, 6.0, (TOKENS, HEADS * HEAD_DIM), jnp.float32)
    return values.astype(jnp.bfloat16)


def draw_stripe(key, part):
    key = jax.random.fold_in(key, 11)
    segments = TOKENS // TOK_DEV
    seg_keys = jax.random.split(key, segments)
    local = jax.vmap(lambda one_key: jax.random.permutation(one_key, TOK_DEV))(seg_keys)
    base = (jnp.arange(segments, dtype=jnp.int32) * TOK_DEV)[:, None]
    return (local.astype(jnp.int32) + base).reshape(TOKENS)


def draw_frame_len(key, part):
    key = jax.random.fold_in(key, 13)
    segments = TOKENS // TOK_DEV
    cuts = jax.random.randint(key, (segments,), 1, TOK_DEV, dtype=jnp.int32)
    cuts = cuts.at[0].set(1).at[1].set(TOK_DEV - 1)
    ends = jnp.arange(segments, dtype=jnp.int32) * TOK_DEV + cuts
    bounds = jnp.concatenate([jnp.zeros((1,), jnp.int32), ends, jnp.full((1,), TOKENS, jnp.int32)])
    return bounds[1:] - bounds[:-1]


def levels(key, extent, cuts, low, largest):
    def one(dim, shards_of):
        heights = jax.random.uniform(jax.random.fold_in(jax.random.fold_in(key, 6), dim), (shards_of,), jnp.float32, low / len(cuts), largest / len(cuts))
        return jnp.repeat(jnp.exp(heights), extent[dim] // shards_of).reshape((-1,) + (1,) * (len(extent) - dim - 1))

    level = one(*cuts[0])
    for cut in cuts[1:]:
        level = level * one(*cut)
    return level


def normal_values(own_key, shape, scale, reach, cuts=(), kind=jnp.bfloat16):
    gain = levels(own_key, shape, cuts, -0.22, 0.18) if cuts else 1.0
    drawn = jax.random.normal(own_key, shape, jnp.float32) * scale * gain
    return jnp.minimum(jnp.maximum(drawn, -reach), reach).astype(kind)


def setup_inputs(seed: int = 0) -> dict:
    streams_of = jax.random.split(jax.random.key(seed), 10)
    return {
        "q_nope": draw_q_nope(jax.random.fold_in(streams_of[9], 71), 0),
        "q_rope": normal_values(streams_of[1], (TOKENS, HEADS * ROPE), 1.0, 6.0, ((0, 128), (1, 4))),
        "latent": normal_values(streams_of[2], (TOKENS, LATENT), 1.0, 6.0, ((0, 128),)),
        "key_rope": normal_values(streams_of[3], (TOKENS, ROPE), 1.0, 6.0, ((0, 128),)),
        "w_key": normal_values(streams_of[4], (LATENT, HEADS * HEAD_DIM), LATENT ** -0.5, 0.25, ((0, 128), (1, 4))),
        "w_value": normal_values(streams_of[5], (LATENT, HEADS * HEAD_DIM), LATENT ** -0.5, 0.25, ((0, 128), (1, 4))),
        "stripe": draw_stripe(jax.random.fold_in(streams_of[9], 71), 0),
        "frame_len": draw_frame_len(jax.random.fold_in(streams_of[9], 71), 0),
        "out_grad": normal_values(streams_of[8], (TOKENS, HEADS * HEAD_DIM), 1.0, 6.0, ((0, 128), (1, 4))),
    }


def frames_of(positions, frame_len):
    starts = jnp.cumsum(frame_len) - frame_len
    return jnp.sum((starts[None, :] <= positions[:, None]).astype(jnp.int32), axis=1) - 1


def rounded(values):
    return lax.optimization_barrier(values.astype(jnp.bfloat16)).astype(jnp.float32)


def reference(q_nope, q_rope, latent, key_rope, w_key, w_value, stripe, frame_len, out_grad):
    softmax_scale = HEAD_QK ** -0.5
    highest = lax.Precision.HIGHEST
    blocks = TOKENS // TOK_DEV
    window_rows = 3 * TOK_DEV
    order = jnp.zeros((TOKENS,), jnp.int32).at[stripe].set(jnp.arange(TOKENS, dtype=jnp.int32))
    key_weight = w_key.astype(jnp.float32)
    value_weight = w_value.astype(jnp.float32)
    lat_pos = latent[order].astype(jnp.float32)
    keys = rounded(jnp.dot(lat_pos, key_weight, precision=highest))
    values = rounded(jnp.dot(lat_pos, value_weight, precision=highest))
    margin = ((TOK_DEV, TOK_DEV), (0, 0))
    keys_pad = jnp.pad(keys, margin)
    values_pad = jnp.pad(values, margin)
    rot_pad = jnp.pad(key_rope[order].astype(jnp.float32), margin)
    q_plain = q_nope[order].astype(jnp.float32).reshape(blocks, TOK_DEV, HEADS, HEAD_DIM)
    q_rot = q_rope[order].astype(jnp.float32).reshape(blocks, TOK_DEV, HEADS, ROPE)
    cot = out_grad[order].astype(jnp.float32).reshape(blocks, TOK_DEV, HEADS, HEAD_DIM)

    def one_block(inputs):
        block, query_plain, query_rot, cotangent = inputs
        first = (block * TOK_DEV).astype(jnp.int32)
        key_pos = first - TOK_DEV + jnp.arange(window_rows, dtype=jnp.int32)
        query_pos = first + jnp.arange(TOK_DEV, dtype=jnp.int32)
        key_valid = (key_pos >= 0) & (key_pos < TOKENS)
        key_frame = frames_of(key_pos, frame_len)
        query_frame = frames_of(query_pos, frame_len)
        allowed = key_valid[None, :] & (key_frame[None, :] <= query_frame[:, None]) & (query_pos[:, None] - key_pos[None, :] < WINDOW)
        key_win = lax.dynamic_slice_in_dim(keys_pad, first, window_rows).reshape(window_rows, HEADS, HEAD_DIM)
        value_win = lax.dynamic_slice_in_dim(values_pad, first, window_rows).reshape(window_rows, HEADS, HEAD_DIM)
        rot_win = lax.dynamic_slice_in_dim(rot_pad, first, window_rows)
        scores = jnp.einsum("thd,khd->htk", query_plain, key_win, precision=highest)
        scores = (scores + jnp.einsum("thr,kr->htk", query_rot, rot_win, precision=highest)) * softmax_scale
        scores = jnp.where(allowed[None], scores, -jnp.inf)
        top_score = jnp.max(scores, axis=2, keepdims=True)
        lse = top_score + jnp.log(jnp.sum(jnp.exp(scores - top_score), axis=2, keepdims=True))
        weights = jnp.exp(scores - lse)
        probs = rounded(weights)
        attended = jnp.einsum("htk,khd->thd", probs, value_win, precision=highest).astype(jnp.bfloat16)
        delta = jnp.sum(cotangent * attended.astype(jnp.float32), axis=2).T
        prob_grad = jnp.einsum("thd,khd->htk", cotangent, value_win, precision=highest)
        score_grad = rounded(weights * (prob_grad - delta[:, :, None]))
        grad_plain = softmax_scale * jnp.einsum("htk,khd->thd", score_grad, key_win, precision=highest)
        grad_rot = softmax_scale * jnp.einsum("htk,kr->thr", score_grad, rot_win, precision=highest)
        key_part = rounded(softmax_scale * jnp.einsum("htk,thd->khd", score_grad, query_plain, precision=highest))
        value_part = rounded(jnp.einsum("htk,thd->khd", probs, cotangent, precision=highest))
        lat_part = jnp.dot(key_part.reshape(window_rows, HEADS * HEAD_DIM), key_weight.T, precision=highest)
        lat_part = lat_part + jnp.dot(value_part.reshape(window_rows, HEADS * HEAD_DIM), value_weight.T, precision=highest)
        rot_part = softmax_scale * jnp.einsum("htk,thr->kr", score_grad, query_rot, precision=highest)
        return attended, grad_plain, grad_rot, lat_part, rot_part

    block_ids = jnp.arange(blocks, dtype=jnp.int32)
    attended, grad_plain, grad_rot, lat_parts, rot_parts = lax.map(one_block, (block_ids, q_plain, q_rot, cot))

    def assemble(parts, width):
        parts = parts.reshape(blocks, 3, TOK_DEV, width)
        empty = jnp.zeros_like(parts[:1, 0])
        from_next = jnp.concatenate([parts[1:, 0], empty], axis=0)
        from_prev = jnp.concatenate([empty, parts[:-1, 2]], axis=0)
        return (parts[:, 1] + from_next + from_prev).reshape(TOKENS, width)

    d_latent = assemble(lat_parts, LATENT)[stripe]
    d_key_rope = assemble(rot_parts, ROPE)[stripe]
    attended = attended.reshape(TOKENS, HEADS * HEAD_DIM)[stripe]
    dq_nope = grad_plain.reshape(TOKENS, HEADS * HEAD_DIM)[stripe]
    dq_rope = grad_rot.reshape(TOKENS, HEADS * ROPE)[stripe]
    return (attended, dq_nope, dq_rope, d_latent, d_key_rope)
```

```python
import jax
import jax.numpy as jnp
from jax import lax
from jax.experimental import pallas as pl
from jax.experimental.pallas import tpu as pltpu
from jax.sharding import PartitionSpec as P

HEAD_QK = 192
WINDOW = 128
SCALE = HEAD_QK ** (-0.5)
MASKED = -1e30

NY, NX, NZ = 8, 4, 4
TOK = 128
LATENT = 512
ROPE = 64
DIM = 128
PAIRS = 8
PAIR = 2 * DIM
JOINED = LATENT + 2 * ROPE
STAGES = 7
LAG = 2

BF16 = jnp.bfloat16
F32 = jnp.float32


def dot(a, b, ca, cb):
    return lax.dot_general(a, b, (((ca,), (cb,)), ((), ())), preferred_element_type=F32)


def kernel(
    q_hbm, qr_hbm, lat_ref, rope_ref, wk_ref, wv_ref, pos_ref, len_ref, o_hbm,
    att_hbm, dq_hbm, dqr_hbm, dlat_ref, drope_ref,
    q_buf, qr_buf, o_buf, att_buf, dq_buf, dqr_buf,
    pack, zbuf, mix, wk, wv, lat_win, rot_win, bias, acc,
    t1_src, t1_dst, t2_src, t2_dst, t3_src, t3_dst, t4, mine,
    in_sem, out_sem, z_send, z_recv, h_send, h_recv, c_send, c_recv, t_send, t_recv,
):
    me = lax.axis_index("ctx")
    head = lax.axis_index("head")
    z = lax.rem(me, NZ)
    x = lax.rem(lax.div(me, NZ), NX)
    y = lax.div(me, NZ * NX)
    core = lax.rem(head, 2)
    z_hi = lax.div(head, 2)

    def at(y_, x_, z_):
        return {"ctx": (y_ * NX + x_) * NZ + z_}

    z_peers = [lax.rem(z + d, NZ) for d in (1, 2, 3)]
    x_peers = [lax.rem(x + d, NX) for d in (1, 2, 3)]
    y_up, y_down = lax.rem(y + 1, NY), lax.rem(y + NY - 1, NY)
    x_up, x_down = x_peers[0], x_peers[2]
    tokens = NY * NX * NZ
    c_next, c_prev = lax.rem(me + 1, tokens), lax.rem(me + tokens - 1, tokens)
    sibling = {"head": z_hi * 2 + (1 - core)}
    partner = {"head": (1 - z_hi) * 2 + core}

    def remote(src, dst, send, recv, device):
        return pltpu.make_async_remote_copy(
            src_ref=src, dst_ref=dst, send_sem=send, recv_sem=recv,
            device_id=device, device_id_type=pl.DeviceIdType.MESH,
        )

    loads = [
        pltpu.make_async_copy(q_hbm, q_buf, in_sem.at[0]),
        pltpu.make_async_copy(qr_hbm, qr_buf, in_sem.at[1]),
        pltpu.make_async_copy(o_hbm, o_buf, in_sem.at[2]),
    ]
    for copy in loads:
        copy.start()

    barrier = pltpu.get_barrier_semaphore()
    greeted = (
        [at(y, x, p) for p in z_peers]
        + [at(y, p, z) for p in x_peers]
        + [at(y_up, x, z), at(y_down, x, z), {"ctx": c_next}, {"ctx": c_prev}, sibling, partner]
    )
    for device in greeted:
        pl.semaphore_signal(barrier, inc=1, device_id=device, device_id_type=pl.DeviceIdType.MESH)

    half = wk_ref.shape[1] // 2
    for q in range(4):
        rows = (wk_ref, wv_ref)[q // 2][...].astype(F32)
        pack[4 * q : 4 * q + 4, :] = rows[:, (q % 2) * half : (q % 2 + 1) * half]
    zbuf[z] = pack[...].astype(BF16)
    lat_win[1] = lat_ref[...]
    rope = rope_ref[...].astype(F32)
    rot_win[1] = jnp.concatenate([rope, rope], axis=1).astype(BF16)

    pl.semaphore_wait(barrier, len(greeted))

    def z_copy(d, slot):
        return remote(zbuf.at[slot], zbuf.at[slot], z_send.at[d], z_recv.at[d], at(y, x, z_peers[d]))

    for d in range(3):
        z_copy(d, z).start()

    halo = [
        remote(lat_win.at[1], lat_win.at[0], h_send.at[0], h_recv.at[0], {"ctx": c_next}),
        remote(lat_win.at[1], lat_win.at[2], h_send.at[1], h_recv.at[1], {"ctx": c_prev}),
        remote(rot_win.at[1], rot_win.at[0], h_send.at[2], h_recv.at[2], {"ctx": c_next}),
        remote(rot_win.at[1], rot_win.at[2], h_send.at[3], h_recv.at[3], {"ctx": c_prev}),
    ]
    for copy in halo:
        copy.start()

    blocks = [lax.rem(me + tokens + b - 1, tokens) for b in range(3)]
    index = lax.broadcasted_iota(jnp.int32, (1, len_ref.shape[1]), 1)
    lengths = len_ref[...]

    def frames(pos, block):
        start = jnp.sum(jnp.where(index <= block, lengths, 0), axis=1, keepdims=True)
        return block + (pos >= start).astype(jnp.int32)

    own = jnp.broadcast_to(pos_ref[pl.ds(me, 1), :], (TOK, TOK))
    own_pos = jnp.transpose(own)
    own_frame = frames(own_pos, me)
    for b in range(3):
        pos = jnp.broadcast_to(pos_ref[pl.ds(blocks[b], 1), :], (TOK, TOK))
        ok = (frames(pos, blocks[b]) <= own_frame) & (own_pos - pos < WINDOW)
        if b == 0:
            ok = ok & jnp.broadcast_to(me > 0, ok.shape)
        if b == 2:
            ok = ok & jnp.broadcast_to(me < tokens - 1, ok.shape)
        bias[:, b * TOK : (b + 1) * TOK] = jnp.where(ok, 0.0, MASKED)
    acc[...] = jnp.zeros_like(acc)

    for d in range(3):
        z_copy(d, z_peers[2 - d]).wait_recv()
    for s in range(NZ):
        piece = zbuf[s].astype(F32)
        for q in range(4):
            mix[q, 4 * s : 4 * s + 4, :] = piece[4 * q : 4 * q + 4, :]
    for j in range(PAIRS):
        lanes = slice((j % 4) * PAIR, (j % 4 + 1) * PAIR)
        wk[j, y, x] = mix[j // 4, :, lanes].astype(BF16)
        wv[j, y, x] = mix[2 + j // 4, :, lanes].astype(BF16)

    up, down = at(y_up, x, z), at(y_down, x, z)
    left, right = at(y, x_down, z), at(y, x_up, z)

    def y_of(steps):
        return lax.rem(y + steps + NY, NY)

    def x_of(steps):
        return lax.rem(x + steps + NX, NX)

    def k_hop(j, sign, depth, offset):
        part = wk.at[j, y_of(offset)]
        if depth == 3:
            part = part.at[0:2] if sign > 0 else part.at[2:4]
        n = 3 + 2 * depth + (0 if sign > 0 else 1)
        return remote(part, part, c_send.at[j, n], c_recv.at[j, n], up if sign > 0 else down)

    def k_x(j, d, offset):
        part = wk.at[j, y, x_of(offset)]
        return remote(part, part, c_send.at[j, d], c_recv.at[j, d], at(y, x_peers[d], z))

    def v_hop(j, sign, depth, offset):
        part = wv.at[j, y_of(offset), x]
        if depth == 3:
            part = part.at[:, 0:DIM] if sign > 0 else part.at[:, DIM:PAIR]
        n = 11 + 2 * depth + (0 if sign > 0 else 1)
        return remote(part, part, c_send.at[j, n], c_recv.at[j, n], up if sign > 0 else down)

    def v_x(j, sign, depth, offset):
        part = wv.at[j, :, x_of(offset)]
        if depth == 1:
            part = wv.at[j, 0:4, x_of(offset)] if sign > 0 else wv.at[j, 4:8, x_of(offset)]
        n = 19 + 2 * depth + (0 if sign > 0 else 1)
        return remote(part, part, c_send.at[j, n], c_recv.at[j, n], right if sign > 0 else left)

    def arrive(make, j, sign, depth):
        make(j, sign, depth, -sign * (depth + 1)).wait_recv()

    def leave(make, j, sign, depth):
        return make(j, sign, depth, -sign * depth)

    def stage(s, j):
        if s == 0:
            for d in range(3):
                k_x(j, d, 0).start()
            for sign in (1, -1):
                leave(v_hop, j, sign, 0).start()
            return
        if s == 1:
            for d in range(3):
                k_x(j, d, -(d + 1)).wait_recv()
            for sign in (1, -1):
                leave(k_hop, j, sign, 0).start()
        elif s <= 5:
            for sign in (1, -1):
                arrive(k_hop, j, sign, s - 2)
                if s <= 4:
                    leave(k_hop, j, sign, s - 1).start()
        if s <= 4:
            for sign in (1, -1):
                arrive(v_hop, j, sign, s - 1)
                if s <= 3:
                    leave(v_hop, j, sign, s).start()
            if s == 4:
                for sign in (1, -1):
                    leave(v_x, j, sign, 0).start()
        elif s == 5:
            for sign in (1, -1):
                arrive(v_x, j, sign, 0)
                leave(v_x, j, sign, 1).start()
        else:
            for sign in (1, -1):
                arrive(v_x, j, sign, 1)

    def outs(j):
        pair = pl.ds(pl.multiple_of(j * PAIR, PAIR), PAIR)
        rot = pl.ds(pl.multiple_of(j * DIM, DIM), DIM)
        return [
            pltpu.make_async_copy(att_buf.at[:, pair], att_hbm.at[:, pair], out_sem.at[j, 0]),
            pltpu.make_async_copy(dq_buf.at[:, pair], dq_hbm.at[:, pair], out_sem.at[j, 1]),
            pltpu.make_async_copy(dqr_buf.at[:, rot], dqr_hbm.at[:, rot], out_sem.at[j, 2]),
        ]

    def compute(j):
        pair = pl.ds(pl.multiple_of(j * PAIR, PAIR), PAIR)
        rot_cols = pl.ds(pl.multiple_of(j * DIM, DIM), DIM)
        window = lat_win[...].reshape(3 * TOK, LATENT)
        rot = rot_win[...].reshape(3 * TOK, 2 * ROPE)
        key_w = wk[j].reshape(LATENT, PAIR)
        value_w = wv[j].reshape(LATENT, PAIR)
        keys = dot(window, key_w, 1, 0).astype(BF16)
        values = dot(window, value_w, 1, 0).astype(BF16)
        q_pair, o_pair, r_pair = q_buf[:, pair], o_buf[:, pair], qr_buf[:, rot_cols]
        first = lax.broadcasted_iota(jnp.int32, (TOK, 2 * ROPE), 1) < ROPE
        blank = jnp.zeros_like(r_pair)
        key_parts, value_parts, attended, grads, rot_grads = [], [], [], [], []
        rot_part = None
        for e in range(2):
            cols = slice(e * DIM, (e + 1) * DIM)
            value, cot = values[:, cols], o_pair[:, cols]
            r_own = jnp.where(first, r_pair, blank) if e == 0 else jnp.where(first, blank, r_pair)
            key_full = jnp.concatenate([keys[:, cols], rot], axis=1)
            query_full = jnp.concatenate([q_pair[:, cols], r_own], axis=1)
            scores = dot(query_full, key_full, 1, 1) * SCALE + bias[...]
            top = jnp.max(scores, axis=1, keepdims=True)
            weights = jnp.exp(scores - top)
            weights = weights * (1.0 / jnp.sum(weights, axis=1, keepdims=True))
            probs = weights.astype(BF16)
            out = dot(probs, value, 1, 0).astype(BF16)
            delta = jnp.sum(cot.astype(F32) * out.astype(F32), axis=1, keepdims=True)
            prob_grad = dot(cot, value, 1, 1)
            score_grad = (weights * (prob_grad - delta)).astype(BF16)
            grad = dot(score_grad, key_full, 1, 0) * SCALE
            key_side = dot(score_grad, query_full, 0, 0) * SCALE
            value_side = dot(probs, cot, 0, 0)
            attended.append(out)
            grads.append(grad[:, :DIM])
            rot_grads.append(grad[:, DIM:])
            key_parts.append(key_side[:, :DIM].astype(BF16))
            value_parts.append(value_side.astype(BF16))
            rot_part = key_side[:, DIM:] if rot_part is None else rot_part + key_side[:, DIM:]
        att_buf[:, pair] = jnp.concatenate(attended, axis=1)
        dq_buf[:, pair] = jnp.concatenate(grads, axis=1)
        dqr_buf[:, rot_cols] = jnp.where(first, rot_grads[0], rot_grads[1])
        back = dot(jnp.concatenate(key_parts, axis=1), key_w, 1, 1)
        back = back + dot(jnp.concatenate(value_parts, axis=1), value_w, 1, 1)
        acc[:, :, :, :LATENT] += back.reshape(3, 2, TOK // 2, LATENT)
        acc[:, :, :, LATENT:] += rot_part.reshape(3, 2, TOK // 2, 2 * ROPE)
        for copy in outs(j):
            copy.start()

    def slot(t, carry):
        for s in reversed(range(STAGES)):
            j = t - LAG * s

            @pl.when((j >= 0) & (j < PAIRS))
            def _(s=s, j=j):
                stage(s, j)

        last = t - LAG * (STAGES - 1)

        @pl.when(last == 0)
        def _():
            for copy in loads:
                copy.wait()
            for copy in halo:
                copy.wait_recv()

        @pl.when(last >= 0)
        def _():
            compute(last)

        return carry

    lax.fori_loop(0, PAIRS + LAG * (STAGES - 1), slot, 0)

    rows = TOK // 2

    def halves(e):
        both = acc[:, e]
        rot = both[:, :, LATENT:].reshape(3 * rows, 2 * ROPE)
        rot = (rot + pltpu.roll(rot, ROPE, 1)).reshape(3, rows, 2 * ROPE)
        return both[:, :, :LATENT], rot

    sent_lat, sent_rot = halves(1 - core)
    t1_src[:, :, :LATENT] = sent_lat.astype(BF16)
    t1_src[:, :, LATENT:] = sent_rot.astype(BF16)
    step1 = remote(t1_src, t1_dst, t_send.at[0], t_recv.at[0], sibling)
    step1.start()
    own_lat, own_rot = halves(core)
    mine[:, :, :LATENT] = own_lat
    mine[:, :, LATENT:] = own_rot
    step1.wait_recv()
    got = t1_dst[...].astype(F32)
    t2_src[0] = (mine[0] + got[0]).astype(BF16)
    t2_src[1] = (mine[2] + got[2]).astype(BF16)
    step2 = [
        remote(t2_src.at[0], t2_dst.at[0], t_send.at[1], t_recv.at[1], {"ctx": c_prev}),
        remote(t2_src.at[1], t2_dst.at[1], t_send.at[2], t_recv.at[2], {"ctx": c_next}),
    ]
    for copy in step2:
        copy.start()
    centre = mine[1] + got[1]
    for copy in step2:
        copy.wait_recv()
    t3_src[...] = (centre + t2_dst[0].astype(F32) + t2_dst[1].astype(F32)).astype(BF16)
    step3 = remote(t3_src, t3_dst, t_send.at[3], t_recv.at[3], partner)
    step3.start()
    step3.wait_recv()
    t4[core] = t3_src[...].astype(F32) + t3_dst[...].astype(F32)
    step4 = remote(t4.at[core], t4.at[core], t_send.at[4], t_recv.at[4], sibling)
    step4.start()
    other = remote(t4.at[1 - core], t4.at[1 - core], t_send.at[4], t_recv.at[4], sibling)
    other.wait_recv()
    whole = t4[...].reshape(TOK, JOINED)
    dlat_ref[...] = whole[:, :LATENT]
    drope_ref[...] = whole[:, LATENT : LATENT + ROPE]

    step1.wait_send()
    for copy in step2:
        copy.wait_send()
    step3.wait_send()
    step4.wait_send()
    for d in range(3):
        z_copy(d, z).wait_send()
    for copy in halo:
        copy.wait_send()

    def drain(j, carry):
        for d in range(3):
            k_x(j, d, 0).wait_send()
        for sign in (1, -1):
            for depth in range(4):
                leave(k_hop, j, sign, depth).wait_send()
                leave(v_hop, j, sign, depth).wait_send()
            for depth in range(2):
                leave(v_x, j, sign, depth).wait_send()
        for copy in outs(j):
            copy.wait()
        return carry

    lax.fori_loop(0, PAIRS, drain, 0)


def on_device(q_nope, q_rope, latent, key_rope, w_key, w_value, stripe, frame_len, out_grad):
    cols = q_nope.shape[1]
    rot_cols = q_rope.shape[1]
    positions = stripe.reshape(-1, TOK)
    lengths = frame_len.reshape(1, -1)
    vmem = pl.BlockSpec(memory_space=pltpu.VMEM)
    hbm = pl.BlockSpec(memory_space=pl.ANY)
    rows = TOK // 2
    copies = 23
    dma = pltpu.SemaphoreType.DMA
    return pl.pallas_call(
        kernel,
        out_shape=(
            jax.ShapeDtypeStruct((TOK, cols), BF16),
            jax.ShapeDtypeStruct((TOK, cols), F32),
            jax.ShapeDtypeStruct((TOK, rot_cols), F32),
            jax.ShapeDtypeStruct((TOK, LATENT), F32),
            jax.ShapeDtypeStruct((TOK, ROPE), F32),
        ),
        in_specs=[hbm, hbm, vmem, vmem, vmem, vmem, vmem, vmem, hbm],
        out_specs=(hbm, hbm, hbm, vmem, vmem),
        scratch_shapes=[
            pltpu.VMEM((TOK, cols), BF16),
            pltpu.VMEM((TOK, rot_cols), BF16),
            pltpu.VMEM((TOK, cols), BF16),
            pltpu.VMEM((TOK, cols), BF16),
            pltpu.VMEM((TOK, cols), F32),
            pltpu.VMEM((TOK, rot_cols), F32),
            pltpu.VMEM((16, cols // 2), F32),
            pltpu.VMEM((NZ, 16, cols // 2), BF16),
            pltpu.VMEM((4, 16, cols // 2), F32),
            pltpu.VMEM((PAIRS, NY, NX, 16, PAIR), BF16),
            pltpu.VMEM((PAIRS, NY, NX, 16, PAIR), BF16),
            pltpu.VMEM((3, TOK, LATENT), BF16),
            pltpu.VMEM((3, TOK, 2 * ROPE), BF16),
            pltpu.VMEM((TOK, 3 * TOK), F32),
            pltpu.VMEM((3, 2, rows, JOINED), F32),
            pltpu.VMEM((3, rows, JOINED), BF16),
            pltpu.VMEM((3, rows, JOINED), BF16),
            pltpu.VMEM((2, rows, JOINED), BF16),
            pltpu.VMEM((2, rows, JOINED), BF16),
            pltpu.VMEM((rows, JOINED), BF16),
            pltpu.VMEM((rows, JOINED), BF16),
            pltpu.VMEM((2, rows, JOINED), F32),
            pltpu.VMEM((3, rows, JOINED), F32),
            dma((3,)),
            dma((PAIRS, 3)),
            dma((3,)),
            dma((3,)),
            dma((4,)),
            dma((4,)),
            dma((PAIRS, copies)),
            dma((PAIRS, copies)),
            dma((5,)),
            dma((5,)),
        ],
        compiler_params=pltpu.CompilerParams(
            collective_id=0, has_side_effects=True, vmem_limit_bytes=48 * 1024 * 1024
        ),
        cost_estimate=pl.CostEstimate(flops=4_700_000_000, bytes_accessed=5_000_000, transcendentals=800_000),
        name="latent_attention",
    )(q_nope, q_rope, latent, key_rope, w_key, w_value, positions, lengths, out_grad)


def solution(mesh):
    return jax.shard_map(
        on_device,
        mesh=mesh,
        in_specs=(
            P("ctx", "head"),
            P("ctx", "head"),
            P("ctx", None),
            P("ctx", None),
            P("ctx", "head"),
            P("ctx", "head"),
            P(),
            P(),
            P("ctx", "head"),
        ),
        out_specs=(
            P("ctx", "head"),
            P("ctx", "head"),
            P("ctx", "head"),
            P("ctx", None),
            P("ctx", None),
        ),
        check_vma=False,
    )
```

```python
import jax
import jax.numpy as jnp
from jax import lax
from jax.experimental import pallas as pl
from jax.experimental.pallas import tpu as pltpu
from jax.sharding import PartitionSpec as P

HEAD_QK = 192
WINDOW = 128
SCALE = HEAD_QK ** (-0.5)
MASKED = -1e30
VMEM_BYTES = 60 * 1024 * 1024

NY, NX, NZ = 8, 4, 4
TOK = 128
LATENT = 512
ROPE = 64
DIM = 128
CHUNKS = 4
WIDTH = 4 * DIM
ROWS = LATENT + ROPE
HALF = ROWS // 2
K_SLOTS = (0, 1, 2, 3, 4)
V_SLOTS = (2, 3, 4)
K_GROUPS = ((0, 1), (1, CHUNKS))
V_GROUP = (1, CHUNKS)

BF16 = jnp.bfloat16
F32 = jnp.float32


def dot(a, b, ca, cb):
    return lax.dot_general(a, b, (((ca,), (cb,)), ((), ())), preferred_element_type=F32)


def kernel(
    q_hbm, qr_hbm, lat_hbm, rope_hbm, wk_ref, wv_ref, pos_hbm, len_ref, o_hbm,
    att_hbm, dq_hbm, dqr_hbm, dlat_ref, drope_ref,
    q_buf, qr_buf, o_buf, rope_buf, pos_ref, att_buf, dq_buf, dqr_buf,
    pack, zbuf, mix, wk, wv, lat_win, rot_win, bias, acc,
    t1_src, t1_dst, t2_src, t2_dst, t3_src, t3_dst, t4,
    in_sem, out_sem, z_send, z_recv, h_send, h_recv, g_send, g_recv, c_send, c_recv, t_send, t_recv,
):
    me = lax.axis_index("ctx")
    head = lax.axis_index("head")
    z = lax.rem(me, NZ)
    x = lax.rem(lax.div(me, NZ), NX)
    y = lax.div(me, NZ * NX)
    core = lax.rem(head, 2)
    z_hi = lax.div(head, 2)

    def at(y_, x_, z_):
        return {"ctx": (y_ * NX + x_) * NZ + z_}

    z_peers = [lax.rem(z + d, NZ) for d in (1, 2, 3)]
    x_peers = [lax.rem(x + d, NX) for d in (1, 2, 3)]
    y_peers = [lax.rem(y + d, NY) for d in range(1, NY)]
    y_up, y_down = y_peers[0], y_peers[-1]
    x_up, x_down = x_peers[0], x_peers[2]
    tokens = NY * NX * NZ
    c_next, c_prev = lax.rem(me + 1, tokens), lax.rem(me + tokens - 1, tokens)
    sibling = {"head": z_hi * 2 + (1 - core)}
    partner = {"head": (1 - z_hi) * 2 + core}

    def remote(src, dst, send, recv, device):
        return pltpu.make_async_remote_copy(
            src_ref=src, dst_ref=dst, send_sem=send, recv_sem=recv,
            device_id=device, device_id_type=pl.DeviceIdType.MESH,
        )

    loads = [
        pltpu.make_async_copy(q_hbm, q_buf, in_sem.at[0]),
        pltpu.make_async_copy(qr_hbm, qr_buf, in_sem.at[1]),
        pltpu.make_async_copy(o_hbm, o_buf, in_sem.at[2]),
    ]
    early = [
        pltpu.make_async_copy(lat_hbm, lat_win.at[1], in_sem.at[3]),
        pltpu.make_async_copy(rope_hbm, rope_buf, in_sem.at[4]),
        pltpu.make_async_copy(pos_hbm, pos_ref, in_sem.at[5]),
    ]
    for copy in early + loads:
        copy.start()

    barrier = pltpu.get_barrier_semaphore()
    greeted = (
        [at(y, x, p) for p in z_peers]
        + [at(y, p, z) for p in x_peers]
        + [at(p, x, z) for p in y_peers]
        + [{"ctx": c_next}, {"ctx": c_prev}, sibling, partner]
    )
    for device in greeted:
        pl.semaphore_signal(barrier, inc=1, device_id=device, device_id_type=pl.DeviceIdType.MESH)

    half = wk_ref.shape[1] // 2
    for q in range(4):
        rows = (wk_ref, wv_ref)[q // 2][...].astype(F32)
        pack[4 * q : 4 * q + 4, :] = rows[:, (q % 2) * half : (q % 2 + 1) * half]
    zbuf[z] = pack[...].astype(BF16)
    for copy in early:
        copy.wait()
    rope = jnp.transpose(rope_buf[...].astype(F32))
    rot_win[1] = jnp.concatenate([rope, rope], axis=1).astype(BF16)

    pl.semaphore_wait(barrier, len(greeted))

    def z_copy(d, slot):
        return remote(zbuf.at[slot], zbuf.at[slot], z_send.at[d], z_recv.at[d], at(y, x, z_peers[d]))

    for d in range(3):
        z_copy(d, z).start()

    blocks = [lax.rem(me + tokens + b - 1, tokens) for b in range(3)]
    index = lax.broadcasted_iota(jnp.int32, (1, len_ref.shape[1]), 1)
    lengths = len_ref[...]

    def frames(pos, block):
        start = jnp.sum(jnp.where(index <= block, lengths, 0), axis=1, keepdims=True)
        return block + (pos >= start).astype(jnp.int32)

    own = jnp.broadcast_to(pos_ref[pl.ds(me, 1), :], (TOK, TOK))
    own_pos = jnp.transpose(own)
    own_frame = frames(own_pos, me)
    for b in range(3):
        pos = jnp.broadcast_to(pos_ref[pl.ds(blocks[b], 1), :], (TOK, TOK))
        ok = (frames(pos, blocks[b]) <= own_frame) & (own_pos - pos < WINDOW)
        if b == 0:
            ok = ok & jnp.broadcast_to(me > 0, ok.shape)
        if b == 2:
            ok = ok & jnp.broadcast_to(me < tokens - 1, ok.shape)
        bias[:, b * TOK : (b + 1) * TOK] = jnp.where(ok, 0.0, MASKED)
    acc[...] = jnp.zeros_like(acc)

    for d in range(3):
        z_copy(d, z_peers[2 - d]).wait_recv()
    for s in range(NZ):
        piece = zbuf[s].astype(F32)
        for q in range(4):
            mix[q, 4 * s : 4 * s + 4, :] = piece[4 * q : 4 * q + 4, :]
    for j in range(CHUNKS):
        lanes = slice((j % 2) * WIDTH, (j % 2 + 1) * WIDTH)
        wk[j, y, x] = mix[j // 2, :, lanes].astype(BF16)
        wv[j, y, x] = mix[2 + j // 2, :, lanes].astype(BF16)

    up, down = at(y_up, x, z), at(y_down, x, z)
    left, right = at(y, x_down, z), at(y, x_up, z)

    def y_of(steps):
        return lax.rem(y + steps + NY, NY)

    def x_of(steps):
        return lax.rem(x + steps + NX, NX)

    def k_x(g, d, offset):
        part = wk.at[slice(*K_GROUPS[g]), y, x_of(offset)]
        n = 3 * g + d
        return remote(part, part, g_send.at[n], g_recv.at[n], at(y, x_peers[d], z))

    def v_direct(d, offset):
        part = wv.at[0, y_of(offset), x]
        n = 6 + d
        return remote(part, part, g_send.at[n], g_recv.at[n], at(y_peers[d], x, z))

    def v_hop(_, sign, depth, offset):
        part = wv.at[slice(*V_GROUP), y_of(offset), x]
        if depth == 3:
            part = part.at[:, :, : WIDTH // 2] if sign > 0 else part.at[:, :, WIDTH // 2 :]
        n = 13 + 2 * depth + (0 if sign > 0 else 1)
        return remote(part, part, g_send.at[n], g_recv.at[n], up if sign > 0 else down)

    def k_hop(j, sign, depth, offset):
        part = wk.at[j, y_of(offset)]
        if depth == 3:
            part = part.at[0:2] if sign > 0 else part.at[2:4]
        n = 2 * depth + (0 if sign > 0 else 1)
        return remote(part, part, c_send.at[j, n], c_recv.at[j, n], up if sign > 0 else down)

    def v_x(j, sign, depth, offset):
        part = wv.at[j, :, x_of(offset)]
        if depth == 1:
            part = wv.at[j, 0:4, x_of(offset)] if sign > 0 else wv.at[j, 4:8, x_of(offset)]
        n = 8 + 2 * depth + (0 if sign > 0 else 1)
        return remote(part, part, c_send.at[j, n], c_recv.at[j, n], right if sign > 0 else left)

    def arrive(make, j, sign, depth):
        make(j, sign, depth, -sign * (depth + 1)).wait_recv()

    def leave(make, j, sign, depth):
        return make(j, sign, depth, -sign * depth)

    def hop(make, j, n, last):
        for sign in (1, -1):
            if n > 0:
                arrive(make, j, sign, n - 1)
            if n < last:
                leave(make, j, sign, n).start()

    for d in range(NY - 1):
        v_direct(d, 0).start()
    for g in range(2):
        for d in range(3):
            k_x(g, d, 0).start()
        if g == 0:
            hop(v_hop, 0, 0, 4)

    halo = [
        remote(lat_win.at[1], lat_win.at[0], h_send.at[0], h_recv.at[0], {"ctx": c_next}),
        remote(lat_win.at[1], lat_win.at[2], h_send.at[1], h_recv.at[1], {"ctx": c_prev}),
        remote(rot_win.at[1], rot_win.at[0], h_send.at[2], h_recv.at[2], {"ctx": c_next}),
        remote(rot_win.at[1], rot_win.at[2], h_send.at[3], h_recv.at[3], {"ctx": c_prev}),
    ]
    for copy in halo:
        copy.start()

    def columns(j, width):
        return pl.ds(pl.multiple_of(j * width, width), width)

    def outs(j):
        plain, rot = columns(j, WIDTH), columns(j, WIDTH // 2)
        return [
            pltpu.make_async_copy(att_buf.at[:, plain], att_hbm.at[:, plain], out_sem.at[j, 0]),
            pltpu.make_async_copy(dq_buf.at[:, plain], dq_hbm.at[:, plain], out_sem.at[j, 1]),
            pltpu.make_async_copy(dqr_buf.at[:, rot], dqr_hbm.at[:, rot], out_sem.at[j, 2]),
        ]

    def compute(j):
        plain, rot_cols = columns(j, WIDTH), columns(j, WIDTH // 2)
        window = lat_win[...].reshape(3 * TOK, LATENT)
        rot = rot_win[...].reshape(3 * TOK, 2 * ROPE)
        key_w = wk[j].reshape(LATENT, WIDTH)
        value_w = wv[j].reshape(LATENT, WIDTH)
        keys = dot(window, key_w, 1, 0).astype(BF16)
        values = dot(window, value_w, 1, 0).astype(BF16)
        queries, cots, rots = q_buf[:, plain], o_buf[:, plain], qr_buf[:, rot_cols]
        first = lax.broadcasted_iota(jnp.int32, (TOK, 2 * ROPE), 1) < ROPE
        blank = jnp.zeros((TOK, 2 * ROPE), BF16)
        key_parts, value_parts, attended, grads, rot_grads = [], [], [], [], []
        rot_part = None
        for e in range(4):
            cols = slice(e * DIM, (e + 1) * DIM)
            value, cot = values[:, cols], cots[:, cols]
            r_pair = rots[:, (e // 2) * DIM : (e // 2 + 1) * DIM]
            r_own = jnp.where(first, r_pair, blank) if e % 2 == 0 else jnp.where(first, blank, r_pair)
            key_full = jnp.concatenate([keys[:, cols], rot], axis=1)
            query_full = jnp.concatenate([queries[:, cols], r_own], axis=1)
            scores = dot(query_full, key_full, 1, 1) * SCALE + bias[...]
            top = jnp.max(scores, axis=1, keepdims=True)
            weights = jnp.exp(scores - top)
            weights = weights * (1.0 / jnp.sum(weights, axis=1, keepdims=True))
            probs = weights.astype(BF16)
            out = dot(probs, value, 1, 0).astype(BF16)
            delta = jnp.sum(cot.astype(F32) * out.astype(F32), axis=1, keepdims=True)
            prob_grad = dot(cot, value, 1, 1)
            score_grad = (weights * (prob_grad - delta)).astype(BF16)
            grad = dot(score_grad, key_full, 1, 0) * SCALE
            key_side = dot(query_full, score_grad, 0, 0) * SCALE
            value_parts.append(dot(cot, probs, 0, 0).astype(BF16))
            key_parts.append(key_side[:DIM].astype(BF16))
            rot_part = key_side[DIM:] if rot_part is None else rot_part + key_side[DIM:]
            attended.append(out)
            grads.append(grad[:, :DIM])
            rot_grads.append(grad[:, DIM:])
        att_buf[:, plain] = jnp.concatenate(attended, axis=1)
        dq_buf[:, plain] = jnp.concatenate(grads, axis=1)
        dqr_buf[:, rot_cols] = jnp.concatenate(
            [jnp.where(first, rot_grads[e], rot_grads[e + 1]) for e in (0, 2)], axis=1
        )
        back = dot(key_w, jnp.concatenate(key_parts, axis=0), 1, 0)
        acc[:LATENT] += back + dot(value_w, jnp.concatenate(value_parts, axis=0), 1, 0)
        acc[LATENT:] += rot_part
        for copy in outs(j):
            copy.start()

    def slot(t, carry):
        def during(j, run):
            @pl.when((j >= 0) & (j < CHUNKS))
            def _():
                run(j)

        def once(when, run):
            @pl.when(t == when)
            def _():
                run()

        def k_arrive(g):
            for d in range(3):
                k_x(g, d, -(d + 1)).wait_recv()

        def v_arrive():
            for d in range(NY - 1):
                v_direct(d, -(d + 1)).wait_recv()

        for n in reversed(range(1, 5)):
            during(t - K_SLOTS[n], lambda j, n=n: hop(k_hop, j, n, 4))
        for n in reversed(range(1, 3)):
            during(t - V_SLOTS[n], lambda j, n=n: hop(v_x, j, n, 2))
        for g in range(2):
            once(g, lambda g=g: k_arrive(g))
        during(t - K_SLOTS[0], lambda j: hop(k_hop, j, 0, 4))
        once(V_SLOTS[0], v_arrive)
        for n in range(1, 5):
            once(n - 1, lambda n=n: hop(v_hop, 0, n, 4))
        during(t - V_SLOTS[0], lambda j: hop(v_x, j, 0, 2))

        last = t - max(K_SLOTS[-1], V_SLOTS[-1])

        @pl.when(last == 0)
        def _():
            for copy in loads:
                copy.wait()
            for copy in halo:
                copy.wait_recv()

        @pl.when(last >= 0)
        def _():
            compute(last)

        return carry

    lax.fori_loop(0, CHUNKS + max(K_SLOTS[-1], V_SLOTS[-1]), slot, 0)

    acc[LATENT:ROWS] += acc[ROWS:]
    t1_src[...] = acc[pl.ds(pl.multiple_of((1 - core) * HALF, HALF), HALF)].astype(BF16)
    step1 = remote(t1_src, t1_dst, t_send.at[0], t_recv.at[0], sibling)
    step1.start()
    mine = acc[pl.ds(pl.multiple_of(core * HALF, HALF), HALF)]
    step1.wait_recv()
    mine = mine + t1_dst[...].astype(F32)
    t2_src[0] = mine[:, :TOK].astype(BF16)
    t2_src[1] = mine[:, 2 * TOK :].astype(BF16)
    step2 = [
        remote(t2_src.at[0], t2_dst.at[0], t_send.at[1], t_recv.at[1], {"ctx": c_prev}),
        remote(t2_src.at[1], t2_dst.at[1], t_send.at[2], t_recv.at[2], {"ctx": c_next}),
    ]
    for copy in step2:
        copy.start()
    for copy in step2:
        copy.wait_recv()
    t3_src[...] = (mine[:, TOK : 2 * TOK] + t2_dst[0].astype(F32) + t2_dst[1].astype(F32)).astype(BF16)
    step3 = remote(t3_src, t3_dst, t_send.at[3], t_recv.at[3], partner)
    step3.start()
    step3.wait_recv()
    t4[core] = t3_src[...].astype(F32) + t3_dst[...].astype(F32)
    step4 = remote(t4.at[core], t4.at[core], t_send.at[4], t_recv.at[4], sibling)
    step4.start()
    other = remote(t4.at[1 - core], t4.at[1 - core], t_send.at[4], t_recv.at[4], sibling)
    other.wait_recv()
    whole = t4[...].reshape(ROWS, TOK)
    dlat_ref[...] = jnp.transpose(whole[:LATENT])
    drope_ref[...] = whole[LATENT:]

    step1.wait_send()
    for copy in step2:
        copy.wait_send()
    step3.wait_send()
    step4.wait_send()
    for d in range(3):
        z_copy(d, z).wait_send()
    for copy in halo:
        copy.wait_send()

    for d in range(NY - 1):
        v_direct(d, 0).wait_send()
    for d in range(3):
        k_x(0, d, 0).wait_send()
        k_x(1, d, 0).wait_send()
    for sign in (1, -1):
        for depth in range(4):
            leave(v_hop, 0, sign, depth).wait_send()

    def drain(j, carry):
        for sign in (1, -1):
            for depth in range(4):
                leave(k_hop, j, sign, depth).wait_send()
            for depth in range(2):
                leave(v_x, j, sign, depth).wait_send()
        for copy in outs(j):
            copy.wait()
        return carry

    lax.fori_loop(0, CHUNKS, drain, 0)


PARTS = (1, 2, 1, 1, 1)


def write_out(*refs):
    count = len(PARTS)
    sources, targets, buffers = refs[:count], refs[count : 2 * count], refs[2 * count : 3 * count]
    came, left = refs[3 * count :]
    moves = []
    for source, target, buffer, parts in zip(sources, targets, buffers, PARTS):
        size = source.shape[0] // parts
        for p in range(parts):
            n = len(moves)
            rows = slice(p * size, (p + 1) * size)
            moves.append((
                pltpu.make_async_copy(source.at[rows], buffer.at[rows], came.at[n]),
                pltpu.make_async_copy(buffer.at[rows], target.at[rows], left.at[n]),
            ))
    for load, _ in moves:
        load.start()
    for load, store in moves:
        load.wait()
        store.start()
    for _, store in moves:
        store.wait()


def on_device(q_nope, q_rope, latent, key_rope, w_key, w_value, stripe, frame_len, out_grad):
    cols = q_nope.shape[1]
    rot_cols = q_rope.shape[1]
    positions = stripe.reshape(-1, TOK)
    lengths = frame_len.reshape(1, -1)
    vmem = pl.BlockSpec(memory_space=pltpu.VMEM)
    hbm = pl.BlockSpec(memory_space=pltpu.HBM)
    dma = pltpu.SemaphoreType.DMA
    outs = (
        jax.ShapeDtypeStruct((TOK, cols), BF16),
        jax.ShapeDtypeStruct((TOK, cols), F32),
        jax.ShapeDtypeStruct((TOK, rot_cols), F32),
        jax.ShapeDtypeStruct((TOK, LATENT), F32),
        jax.ShapeDtypeStruct((ROPE, TOK), F32),
    )
    results = pl.pallas_call(
        kernel,
        out_shape=outs,
        in_specs=[hbm, hbm, hbm, hbm, vmem, vmem, hbm, vmem, hbm],
        out_specs=(hbm, hbm, hbm, vmem, vmem),
        scratch_shapes=[
            pltpu.VMEM((TOK, cols), BF16),
            pltpu.VMEM((TOK, rot_cols), BF16),
            pltpu.VMEM((TOK, cols), BF16),
            pltpu.VMEM((ROPE, TOK), BF16),
            pltpu.VMEM(positions.shape, jnp.int32),
            pltpu.VMEM((TOK, cols), BF16),
            pltpu.VMEM((TOK, cols), F32),
            pltpu.VMEM((TOK, rot_cols), F32),
            pltpu.VMEM((16, cols // 2), F32),
            pltpu.VMEM((NZ, 16, cols // 2), BF16),
            pltpu.VMEM((4, 16, cols // 2), F32),
            pltpu.VMEM((CHUNKS, NY, NX, 16, WIDTH), BF16),
            pltpu.VMEM((CHUNKS, NY, NX, 16, WIDTH), BF16),
            pltpu.VMEM((3, TOK, LATENT), BF16),
            pltpu.VMEM((3, TOK, 2 * ROPE), BF16),
            pltpu.VMEM((TOK, 3 * TOK), F32),
            pltpu.VMEM((LATENT + 2 * ROPE, 3 * TOK), F32),
            pltpu.VMEM((HALF, 3 * TOK), BF16),
            pltpu.VMEM((HALF, 3 * TOK), BF16),
            pltpu.VMEM((2, HALF, TOK), BF16),
            pltpu.VMEM((2, HALF, TOK), BF16),
            pltpu.VMEM((HALF, TOK), BF16),
            pltpu.VMEM((HALF, TOK), BF16),
            pltpu.VMEM((2, HALF, TOK), F32),
            dma((6,)),
            dma((CHUNKS, 3)),
            dma((3,)),
            dma((3,)),
            dma((4,)),
            dma((4,)),
            dma((21,)),
            dma((21,)),
            dma((CHUNKS, 12)),
            dma((CHUNKS, 12)),
            dma((5,)),
            dma((5,)),
        ],
        compiler_params=pltpu.CompilerParams(
            collective_id=0, has_side_effects=True, vmem_limit_bytes=VMEM_BYTES
        ),
        cost_estimate=pl.CostEstimate(flops=4_700_000_000, bytes_accessed=5_000_000, transcendentals=800_000),
        name="latent_attention",
    )(q_nope, q_rope, latent, key_rope.T, w_key, w_value, positions, lengths, out_grad)
    attended, dq_nope, dq_rope, d_latent, d_key_rope = pl.pallas_call(
        write_out,
        out_shape=outs,
        in_specs=[hbm] * len(outs),
        out_specs=(hbm,) * len(outs),
        compiler_params=pltpu.CompilerParams(vmem_limit_bytes=VMEM_BYTES),
        scratch_shapes=[pltpu.VMEM(out.shape, out.dtype) for out in outs] + [dma((sum(PARTS),))] * 2,
        name="write_out",
    )(*results)
    return attended, dq_nope, dq_rope, d_latent, d_key_rope.T


def solution(mesh):
    return jax.shard_map(
        on_device,
        mesh=mesh,
        in_specs=(
            P("ctx", "head"),
            P("ctx", "head"),
            P("ctx", None),
            P("ctx", None),
            P("ctx", "head"),
            P("ctx", "head"),
            P(),
            P(),
            P("ctx", "head"),
        ),
        out_specs=(
            P("ctx", "head"),
            P("ctx", "head"),
            P("ctx", "head"),
            P("ctx", None),
            P("ctx", None),
        ),
        check_vma=False,
    )
```

```python
import jax
import jax.numpy as jnp
from jax import lax
from jax.experimental import pallas as pl
from jax.experimental.pallas import tpu as pltpu
from jax.sharding import PartitionSpec as P

HEAD_QK = 192
WINDOW = 128
SCALE = HEAD_QK ** (-0.5)
MASKED = -1e30
VMEM_BYTES = 60 * 1024 * 1024

NY, NX, NZ = 8, 4, 4
TOK = 128
LATENT = 512
ROPE = 64
DIM = 128
CHUNKS = 8
WIDTH = 2 * DIM
STEPS = CHUNKS // 2
HEADS = 4
PIECES = 2
ROWS = LATENT + ROPE
HALF = ROWS // 2
PIECE = HALF // PIECES
K_SLOTS = (0, 3, 5, 7, 9)
V_SLOTS = (4, 6, 9)
K_GROUPS = ((0, 1), (1, CHUNKS))
DIRECT = 2
V_GROUP = (DIRECT, CHUNKS)
V_HOPS = (0, 2, 4, 6)
LAST = max(K_SLOTS[-1], V_SLOTS[-1])

BF16 = jnp.bfloat16
F32 = jnp.float32


def dot(a, b, ca, cb):
    return lax.dot_general(a, b, (((ca,), (cb,)), ((), ())), preferred_element_type=F32)


def kernel(
    q_hbm, qr_hbm, lat_hbm, rope_hbm, wk_hbm, wv_hbm, pos_hbm, len_hbm, o_hbm,
    att_hbm, dq_hbm, dqr_hbm, dlat_ref, drope_ref,
    q_buf, qr_buf, o_buf, rope_buf, pos_ref, wk_ref, wv_ref, len_ref, att_buf, dq_buf, dqr_buf,
    pack, zbuf, mix, wk, wv, lat_win, rot_win, bias, acc,
    t1_src, t1_dst, t2_src, t2_dst, t3_src, t3_dst, t4,
    in_sem, out_sem, z_send, z_recv, h_send, h_recv, g_send, g_recv, c_send, c_recv, t_send, t_recv,
):
    me = lax.axis_index("ctx")
    head = lax.axis_index("head")
    z = lax.rem(me, NZ)
    x = lax.rem(lax.div(me, NZ), NX)
    y = lax.div(me, NZ * NX)
    core = lax.rem(head, 2)
    z_hi = lax.div(head, 2)

    def at(y_, x_, z_):
        return {"ctx": (y_ * NX + x_) * NZ + z_}

    z_peers = [lax.rem(z + d, NZ) for d in (1, 2, 3)]
    x_peers = [lax.rem(x + d, NX) for d in (1, 2, 3)]
    y_peers = [lax.rem(y + d, NY) for d in range(1, NY)]
    y_up, y_down = y_peers[0], y_peers[-1]
    x_up, x_down = x_peers[0], x_peers[2]
    tokens = NY * NX * NZ
    c_next, c_prev = lax.rem(me + 1, tokens), lax.rem(me + tokens - 1, tokens)
    sibling = {"head": z_hi * 2 + (1 - core)}
    partner = {"head": (1 - z_hi) * 2 + core}

    def remote(src, dst, send, recv, device):
        return pltpu.make_async_remote_copy(
            src_ref=src, dst_ref=dst, send_sem=send, recv_sem=recv,
            device_id=device, device_id_type=pl.DeviceIdType.MESH,
        )

    barrier = pltpu.get_barrier_semaphore()
    greeted = (
        [at(y, x, p) for p in z_peers]
        + [at(y, p, z) for p in x_peers]
        + [at(p, x, z) for p in y_peers]
        + [{"ctx": c_next}, {"ctx": c_prev}, sibling, partner]
    )
    for device in greeted:
        pl.semaphore_signal(barrier, inc=1, device_id=device, device_id_type=pl.DeviceIdType.MESH)

    loads = [
        pltpu.make_async_copy(q_hbm, q_buf, in_sem.at[0]),
        pltpu.make_async_copy(qr_hbm, qr_buf, in_sem.at[1]),
        pltpu.make_async_copy(o_hbm, o_buf, in_sem.at[2]),
    ]
    weights = [
        pltpu.make_async_copy(wk_hbm, wk_ref, in_sem.at[6]),
        pltpu.make_async_copy(wv_hbm, wv_ref, in_sem.at[7]),
    ]
    early = [
        pltpu.make_async_copy(len_hbm, len_ref, in_sem.at[8]),
        pltpu.make_async_copy(lat_hbm, lat_win.at[1], in_sem.at[3]),
        pltpu.make_async_copy(rope_hbm, rope_buf, in_sem.at[4]),
        pltpu.make_async_copy(pos_hbm, pos_ref, in_sem.at[5]),
    ]
    for copy in weights + early + loads:
        copy.start()
    for copy in weights:
        copy.wait()

    half = wk_ref.shape[1] // 2
    for q in range(4):
        rows = (wk_ref, wv_ref)[q // 2][...].astype(F32)
        pack[4 * q : 4 * q + 4, :] = rows[:, (q % 2) * half : (q % 2 + 1) * half]
    zbuf[z] = pack[...].astype(BF16)
    pl.semaphore_wait(barrier, len(greeted))

    def z_copy(d, slot):
        return remote(zbuf.at[slot], zbuf.at[slot], z_send.at[d], z_recv.at[d], at(y, x, z_peers[d]))

    for d in range(3):
        z_copy(d, z).start()

    for copy in early:
        copy.wait()
    rope = jnp.transpose(rope_buf[...].astype(F32))
    rot_win[1] = jnp.concatenate([rope, rope], axis=1).astype(BF16)

    blocks = [lax.rem(me + tokens + b - 1, tokens) for b in range(3)]
    index = lax.broadcasted_iota(jnp.int32, (1, len_ref.shape[1]), 1)
    lengths = len_ref[...]

    def frames(pos, block):
        start = jnp.sum(jnp.where(index <= block, lengths, 0), axis=1, keepdims=True)
        return block + (pos >= start).astype(jnp.int32)

    own = jnp.broadcast_to(pos_ref[pl.ds(me, 1), :], (TOK, TOK))
    own_pos = jnp.transpose(own)
    own_frame = frames(own_pos, me)
    for b in range(3):
        pos = jnp.broadcast_to(pos_ref[pl.ds(blocks[b], 1), :], (TOK, TOK))
        ok = (frames(pos, blocks[b]) <= own_frame) & (own_pos - pos < WINDOW)
        if b == 0:
            ok = ok & jnp.broadcast_to(me > 0, ok.shape)
        if b == 2:
            ok = ok & jnp.broadcast_to(me < tokens - 1, ok.shape)
        bias[:, b * TOK : (b + 1) * TOK] = jnp.where(ok, 0.0, MASKED)
    acc[...] = jnp.zeros_like(acc)

    for d in range(3):
        z_copy(d, z_peers[2 - d]).wait_recv()
    for s in range(NZ):
        piece = zbuf[s].astype(F32)
        for q in range(4):
            mix[q, 4 * s : 4 * s + 4, :] = piece[4 * q : 4 * q + 4, :]
    for j in range(CHUNKS):
        lanes = slice((j % 4) * WIDTH, (j % 4 + 1) * WIDTH)
        wk[j, y, x] = mix[j // 4, :, lanes].astype(BF16)
        wv[j, y, x] = mix[2 + j // 4, :, lanes].astype(BF16)

    up, down = at(y_up, x, z), at(y_down, x, z)
    left, right = at(y, x_down, z), at(y, x_up, z)

    def y_of(steps):
        return lax.rem(y + steps + NY, NY)

    def x_of(steps):
        return lax.rem(x + steps + NX, NX)

    def k_x(g, d, offset):
        part = wk.at[slice(*K_GROUPS[g]), y, x_of(offset)]
        n = 3 * g + d
        return remote(part, part, g_send.at[n], g_recv.at[n], at(y, x_peers[d], z))

    def v_direct(d, offset):
        part = wv.at[0:DIRECT, y_of(offset), x]
        n = 6 + d
        return remote(part, part, g_send.at[n], g_recv.at[n], at(y_peers[d], x, z))

    def v_hop(_, sign, depth, offset):
        part = wv.at[slice(*V_GROUP), y_of(offset), x]
        if depth == 3:
            part = part.at[:, :, : WIDTH // 2] if sign > 0 else part.at[:, :, WIDTH // 2 :]
        n = 13 + 2 * depth + (0 if sign > 0 else 1)
        return remote(part, part, g_send.at[n], g_recv.at[n], up if sign > 0 else down)

    def k_hop(j, sign, depth, offset):
        part = wk.at[j, y_of(offset)]
        if depth == 3:
            part = part.at[0:2] if sign > 0 else part.at[2:4]
        n = 2 * depth + (0 if sign > 0 else 1)
        return remote(part, part, c_send.at[j, n], c_recv.at[j, n], up if sign > 0 else down)

    def v_x(j, sign, depth, offset):
        part = wv.at[j, :, x_of(offset)]
        if depth == 1:
            part = wv.at[j, 0:4, x_of(offset)] if sign > 0 else wv.at[j, 4:8, x_of(offset)]
        n = 8 + 2 * depth + (0 if sign > 0 else 1)
        return remote(part, part, c_send.at[j, n], c_recv.at[j, n], right if sign > 0 else left)

    def arrive(make, j, sign, depth):
        make(j, sign, depth, -sign * (depth + 1)).wait_recv()

    def leave(make, j, sign, depth):
        return make(j, sign, depth, -sign * depth)

    def hop(make, j, n, last):
        for sign in (1, -1):
            if n > 0:
                arrive(make, j, sign, n - 1)
            if n < last:
                leave(make, j, sign, n).start()

    for d in range(NY - 1):
        v_direct(d, 0).start()
    for g in range(2):
        for d in range(3):
            k_x(g, d, 0).start()
        if g == 0:
            hop(v_hop, 0, 0, 4)

    halo = [
        remote(lat_win.at[1], lat_win.at[0], h_send.at[0], h_recv.at[0], {"ctx": c_next}),
        remote(lat_win.at[1], lat_win.at[2], h_send.at[1], h_recv.at[1], {"ctx": c_prev}),
        remote(rot_win.at[1], rot_win.at[0], h_send.at[2], h_recv.at[2], {"ctx": c_next}),
        remote(rot_win.at[1], rot_win.at[2], h_send.at[3], h_recv.at[3], {"ctx": c_prev}),
    ]
    for copy in halo:
        copy.start()

    def columns(j, width):
        return pl.ds(pl.multiple_of(j * width, width), width)

    def outs(i):
        plain, rot = columns(i, HEADS * DIM), columns(i, HEADS * ROPE)
        return [
            pltpu.make_async_copy(att_buf.at[:, plain], att_hbm.at[:, plain], out_sem.at[i, 0]),
            pltpu.make_async_copy(dq_buf.at[:, plain], dq_hbm.at[:, plain], out_sem.at[i, 1]),
            pltpu.make_async_copy(dqr_buf.at[:, rot], dqr_hbm.at[:, rot], out_sem.at[i, 2]),
        ]

    def both(ref, i):
        return jnp.concatenate([ref[2 * i + k].reshape(LATENT, WIDTH) for k in range(2)], axis=1)

    def compute(i):
        plain, rot_cols = columns(i, HEADS * DIM), columns(i, HEADS * ROPE)
        every = range(HEADS)
        cols = [slice(e * DIM, (e + 1) * DIM) for e in every]
        window = lat_win[...].reshape(3 * TOK, LATENT)
        rot = rot_win[...].reshape(3 * TOK, 2 * ROPE)
        key_w = both(wk, i)
        keys = dot(window, key_w, 1, 0).astype(BF16)
        queries, rots = q_buf[:, plain], qr_buf[:, rot_cols]
        first = lax.broadcasted_iota(jnp.int32, (TOK, 2 * ROPE), 1) < ROPE
        blank = jnp.zeros((TOK, 2 * ROPE), BF16)
        key, query = [], []
        for e in every:
            r_pair = rots[:, cols[e // 2]]
            r_own = jnp.where(first, r_pair, blank) if e % 2 == 0 else jnp.where(first, blank, r_pair)
            key.append(jnp.concatenate([keys[:, cols[e]], rot], axis=1))
            query.append(jnp.concatenate([queries[:, cols[e]], r_own], axis=1))
        scores = [dot(query[e], key[e], 1, 1) for e in every]
        value_w = both(wv, i)
        values = dot(window, value_w, 1, 0).astype(BF16)
        value = [values[:, cols[e]] for e in every]
        cots = o_buf[:, plain]
        cot = [cots[:, cols[e]] for e in every]
        mask = bias[...]
        weights = []
        for e in every:
            score = scores[e] * SCALE + mask
            top = jnp.max(score, axis=1, keepdims=True)
            weight = jnp.exp(score - top)
            weights.append(weight * (1.0 / jnp.sum(weight, axis=1, keepdims=True)))
        prob_grad = [dot(cot[e], value[e], 1, 1) for e in every]
        probs = [weight.astype(BF16) for weight in weights]
        out = [dot(probs[e], value[e], 1, 0).astype(BF16) for e in every]
        value_side = [dot(cot[e], probs[e], 0, 0).astype(BF16) for e in every]
        delta = [jnp.sum(cot[e].astype(F32) * out[e].astype(F32), axis=1, keepdims=True) for e in every]
        score_grad = [(weights[e] * (prob_grad[e] - delta[e])).astype(BF16) for e in every]
        key_side = [dot(query[e], score_grad[e], 0, 0) * SCALE for e in every]
        grad = [dot(score_grad[e], key[e], 1, 0) * SCALE for e in every]
        key_part = [side[:DIM].astype(BF16) for side in key_side]
        att_buf[:, plain] = jnp.concatenate(out, axis=1)
        dq_buf[:, plain] = jnp.concatenate([g[:, :DIM] for g in grad], axis=1)
        dqr_buf[:, rot_cols] = jnp.concatenate(
            [jnp.where(first, grad[e][:, DIM:], grad[e + 1][:, DIM:]) for e in range(0, HEADS, 2)], axis=1
        )
        back = dot(key_w, jnp.concatenate(key_part, axis=0), 1, 0)
        acc[:LATENT] += back + dot(value_w, jnp.concatenate(value_side, axis=0), 1, 0)
        acc[LATENT:] += sum(side[DIM:] for side in key_side[1:]) + key_side[0][DIM:]
        for copy in outs(i):
            copy.start()

    def slot(t, carry):
        def during(j, run):
            @pl.when((j >= 0) & (j < CHUNKS))
            def _():
                run(j)

        def once(when, run):
            @pl.when(t == when)
            def _():
                run()

        def k_arrive(g):
            for d in range(3):
                k_x(g, d, -(d + 1)).wait_recv()

        def v_arrive():
            for d in range(NY - 1):
                v_direct(d, -(d + 1)).wait_recv()

        for n in reversed(range(1, 5)):
            during(t - K_SLOTS[n], lambda j, n=n: hop(k_hop, j, n, 4))
        for n in reversed(range(1, 3)):
            during(t - V_SLOTS[n], lambda j, n=n: hop(v_x, j, n, 2))
        for g in range(2):
            once(K_GROUPS[g][0], lambda g=g: k_arrive(g))
        during(t - K_SLOTS[0], lambda j: hop(k_hop, j, 0, 4))
        once(V_SLOTS[0], v_arrive)
        for n in range(1, 5):
            once(V_HOPS[n - 1], lambda n=n: hop(v_hop, 0, n, 4))
        during(t - V_SLOTS[0], lambda j: hop(v_x, j, 0, 2))

        @pl.when(t == LAST + 1)
        def _():
            for copy in loads:
                copy.wait()
            for copy in halo:
                copy.wait_recv()

        @pl.when((t > LAST) & (lax.rem(t - LAST, 2) == 1))
        def _():
            compute(lax.div(t - LAST, 2))

        return carry

    lax.fori_loop(0, CHUNKS + LAST, slot, 0)

    acc[LATENT:ROWS] += acc[ROWS:]
    pieces = range(PIECES)

    def rows(owner, p):
        return pl.ds(pl.multiple_of(owner * HALF + p * PIECE, 16), PIECE)

    step1 = [remote(t1_src.at[p], t1_dst.at[p], t_send.at[p, 0], t_recv.at[p, 0], sibling) for p in pieces]
    step2 = [
        [
            remote(t2_src.at[p, k], t2_dst.at[p, k], t_send.at[p, 1 + k], t_recv.at[p, 1 + k], {"ctx": target})
            for k, target in enumerate((c_prev, c_next))
        ]
        for p in pieces
    ]
    step3 = [remote(t3_src.at[p], t3_dst.at[p], t_send.at[p, 3], t_recv.at[p, 3], partner) for p in pieces]

    def step4(owner, p):
        return remote(t4.at[owner, p], t4.at[owner, p], t_send.at[p, 4], t_recv.at[p, 4], sibling)

    for p in pieces:
        t1_src[p] = acc[rows(1 - core, p)].astype(BF16)
        step1[p].start()
    centre = []
    for p in pieces:
        step1[p].wait_recv()
        mine = acc[rows(core, p)] + t1_dst[p].astype(F32)
        t2_src[p, 0] = mine[:, :TOK].astype(BF16)
        t2_src[p, 1] = mine[:, 2 * TOK :].astype(BF16)
        for copy in step2[p]:
            copy.start()
        centre.append(mine[:, TOK : 2 * TOK])

    for d in range(3):
        z_copy(d, z).wait_send()
    for copy in halo:
        copy.wait_send()
    for d in range(NY - 1):
        v_direct(d, 0).wait_send()
    for g in range(2):
        for d in range(3):
            k_x(g, d, 0).wait_send()
    for sign in (1, -1):
        for depth in range(4):
            leave(v_hop, 0, sign, depth).wait_send()

    def drain(j, carry):
        for sign in (1, -1):
            for depth in range(4):
                leave(k_hop, j, sign, depth).wait_send()
            for depth in range(2):
                leave(v_x, j, sign, depth).wait_send()
        return carry

    lax.fori_loop(0, CHUNKS, drain, 0)

    def drain_outs(i, carry):
        for copy in outs(i):
            copy.wait()
        return carry

    lax.fori_loop(0, STEPS, drain_outs, 0)

    for p in pieces:
        for copy in step2[p]:
            copy.wait_recv()
        t3_src[p] = (centre[p] + t2_dst[p, 0].astype(F32) + t2_dst[p, 1].astype(F32)).astype(BF16)
        step3[p].start()
    for p in pieces:
        step3[p].wait_recv()
        t4[core, p] = t3_src[p].astype(F32) + t3_dst[p].astype(F32)
        step4(core, p).start()
    for p in pieces:
        step4(1 - core, p).wait_recv()
    whole = t4[...].reshape(ROWS, TOK)
    dlat_ref[...] = jnp.transpose(whole[:LATENT])
    drope_ref[...] = whole[LATENT:]
    for p in pieces:
        for copy in [step1[p], *step2[p], step3[p], step4(core, p)]:
            copy.wait_send()


PARTS = (2, 4, 2, 1, 1)


def write_out(*refs):
    count = len(PARTS)
    sources, targets, buffers = refs[:count], refs[count : 2 * count], refs[2 * count : 3 * count]
    came, left = refs[3 * count :]
    moves = []
    for source, target, buffer, parts in zip(sources, targets, buffers, PARTS):
        size = source.shape[0] // parts
        for p in range(parts):
            n = len(moves)
            rows = slice(p * size, (p + 1) * size)
            moves.append((
                pltpu.make_async_copy(source.at[rows], buffer.at[rows], came.at[n]),
                pltpu.make_async_copy(buffer.at[rows], target.at[rows], left.at[n]),
            ))
    for load, _ in moves:
        load.start()
    for load, store in moves:
        load.wait()
        store.start()
    for _, store in moves:
        store.wait()


def on_device(q_nope, q_rope, latent, key_rope, w_key, w_value, stripe, frame_len, out_grad):
    cols = q_nope.shape[1]
    rot_cols = q_rope.shape[1]
    positions = stripe.reshape(-1, TOK)
    lengths = frame_len.reshape(1, -1)
    vmem = pl.BlockSpec(memory_space=pltpu.VMEM)
    hbm = pl.BlockSpec(memory_space=pltpu.HBM)
    dma = pltpu.SemaphoreType.DMA
    outs = (
        jax.ShapeDtypeStruct((TOK, cols), BF16),
        jax.ShapeDtypeStruct((TOK, cols), F32),
        jax.ShapeDtypeStruct((TOK, rot_cols), F32),
        jax.ShapeDtypeStruct((TOK, LATENT), F32),
        jax.ShapeDtypeStruct((ROPE, TOK), F32),
    )
    results = pl.pallas_call(
        kernel,
        out_shape=outs,
        in_specs=[hbm] * 9,
        out_specs=(hbm, hbm, hbm, vmem, vmem),
        scratch_shapes=[
            pltpu.VMEM((TOK, cols), BF16),
            pltpu.VMEM((TOK, rot_cols), BF16),
            pltpu.VMEM((TOK, cols), BF16),
            pltpu.VMEM((ROPE, TOK), BF16),
            pltpu.VMEM(positions.shape, jnp.int32),
            pltpu.VMEM(w_key.shape, BF16),
            pltpu.VMEM(w_value.shape, BF16),
            pltpu.VMEM(lengths.shape, jnp.int32),
            pltpu.VMEM((TOK, cols), BF16),
            pltpu.VMEM((TOK, cols), F32),
            pltpu.VMEM((TOK, rot_cols), F32),
            pltpu.VMEM((16, cols // 2), F32),
            pltpu.VMEM((NZ, 16, cols // 2), BF16),
            pltpu.VMEM((4, 16, cols // 2), F32),
            pltpu.VMEM((CHUNKS, NY, NX, 16, WIDTH), BF16),
            pltpu.VMEM((CHUNKS, NY, NX, 16, WIDTH), BF16),
            pltpu.VMEM((3, TOK, LATENT), BF16),
            pltpu.VMEM((3, TOK, 2 * ROPE), BF16),
            pltpu.VMEM((TOK, 3 * TOK), F32),
            pltpu.VMEM((LATENT + 2 * ROPE, 3 * TOK), F32),
            pltpu.VMEM((PIECES, PIECE, 3 * TOK), BF16),
            pltpu.VMEM((PIECES, PIECE, 3 * TOK), BF16),
            pltpu.VMEM((PIECES, 2, PIECE, TOK), BF16),
            pltpu.VMEM((PIECES, 2, PIECE, TOK), BF16),
            pltpu.VMEM((PIECES, PIECE, TOK), BF16),
            pltpu.VMEM((PIECES, PIECE, TOK), BF16),
            pltpu.VMEM((2, PIECES, PIECE, TOK), F32),
            dma((9,)),
            dma((STEPS, 3)),
            dma((3,)),
            dma((3,)),
            dma((4,)),
            dma((4,)),
            dma((21,)),
            dma((21,)),
            dma((CHUNKS, 12)),
            dma((CHUNKS, 12)),
            dma((PIECES, 5)),
            dma((PIECES, 5)),
        ],
        compiler_params=pltpu.CompilerParams(
            collective_id=0, has_side_effects=True, vmem_limit_bytes=VMEM_BYTES
        ),
        cost_estimate=pl.CostEstimate(flops=4_700_000_000, bytes_accessed=5_000_000, transcendentals=800_000),
        name="latent_attention",
    )(q_nope, q_rope, latent, key_rope.T, w_key, w_value, positions, lengths, out_grad)
    attended, dq_nope, dq_rope, d_latent, d_key_rope = pl.pallas_call(
        write_out,
        out_shape=outs,
        in_specs=[hbm] * len(outs),
        out_specs=(hbm,) * len(outs),
        compiler_params=pltpu.CompilerParams(vmem_limit_bytes=VMEM_BYTES),
        scratch_shapes=[pltpu.VMEM(out.shape, out.dtype) for out in outs] + [dma((sum(PARTS),))] * 2,
        name="write_out",
    )(*results)
    return attended, dq_nope, dq_rope, d_latent, d_key_rope.T


def solution(mesh):
    return jax.shard_map(
        on_device,
        mesh=mesh,
        in_specs=(
            P("ctx", "head"),
            P("ctx", "head"),
            P("ctx", None),
            P("ctx", None),
            P("ctx", "head"),
            P("ctx", "head"),
            P(),
            P(),
            P("ctx", "head"),
        ),
        out_specs=(
            P("ctx", "head"),
            P("ctx", "head"),
            P("ctx", "head"),
            P("ctx", None),
            P("ctx", None),
        ),
        check_vma=False,
    )
```

```python
import jax
import jax.numpy as jnp
from jax import lax
from jax.experimental import pallas as pl
from jax.experimental.pallas import tpu as pltpu
from jax.sharding import PartitionSpec as P

HEAD_QK = 192
WINDOW = 128
SCALE = HEAD_QK ** (-0.5)
MASKED = -1e30
VMEM_BYTES = 60 * 1024 * 1024

NY, NX, NZ = 8, 4, 4
TOK = 128
LATENT = 512
ROPE = 64
DIM = 128
CHUNKS = 8
WIDTH = 2 * DIM
STEPS = CHUNKS // 2
HEADS = 4
PIECES = 2
ROWS = LATENT + ROPE
HALF = ROWS // 2
PIECE = HALF // PIECES
K_SLOTS = (0, 3, 5, 7, 9)
V_SLOTS = (3, 6, 8)
K_GROUPS = ((0, 1), (1, CHUNKS))
DIRECT = 3
V_GROUP = (DIRECT, CHUNKS)
V_HOPS = (1, 3, 5, 6)
LAST = max(K_SLOTS[-1], V_SLOTS[-1])

BF16 = jnp.bfloat16
F32 = jnp.float32


def dot(a, b, ca, cb):
    return lax.dot_general(a, b, (((ca,), (cb,)), ((), ())), preferred_element_type=F32)


def kernel(
    q_hbm, qr_hbm, lat_hbm, rope_hbm, wk_hbm, wv_hbm, pos_hbm, len_hbm, o_hbm,
    att_hbm, dq_hbm, dqr_hbm, dlat_ref, drope_ref,
    q_buf, qr_buf, o_buf, rope_buf, pos_ref, wk_ref, wv_ref, len_ref, att_buf, dq_buf, dqr_buf,
    pack, zbuf, mix, wk, wv, lat_win, rot_win, bias, acc,
    t1_src, t1_dst, t2_src, t2_dst, w_dst, t3_src, t3_dst, t4,
    in_sem, out_sem, z_send, z_recv, h_send, h_recv, g_send, g_recv, c_send, c_recv, t_send, t_recv, w_send, w_recv,
):
    me = lax.axis_index("ctx")
    head = lax.axis_index("head")
    z = lax.rem(me, NZ)
    x = lax.rem(lax.div(me, NZ), NX)
    y = lax.div(me, NZ * NX)
    core = lax.rem(head, 2)
    z_hi = lax.div(head, 2)

    def at(y_, x_, z_):
        return {"ctx": (y_ * NX + x_) * NZ + z_}

    z_peers = [lax.rem(z + d, NZ) for d in (1, 2, 3)]
    x_peers = [lax.rem(x + d, NX) for d in (1, 2, 3)]
    y_peers = [lax.rem(y + d, NY) for d in range(1, NY)]
    y_up, y_down = y_peers[0], y_peers[-1]
    x_up, x_down = x_peers[0], x_peers[2]
    tokens = NY * NX * NZ
    c_next, c_prev = lax.rem(me + 1, tokens), lax.rem(me + tokens - 1, tokens)
    sibling = {"head": z_hi * 2 + (1 - core)}
    partner = {"head": (1 - z_hi) * 2 + core}
    first_z, last_z = z == 0, z == NZ - 1

    def remote(src, dst, send, recv, device):
        return pltpu.make_async_remote_copy(
            src_ref=src, dst_ref=dst, send_sem=send, recv_sem=recv,
            device_id=device, device_id_type=pl.DeviceIdType.MESH,
        )

    t2_dst[...] = jnp.zeros_like(t2_dst)
    w_dst[...] = jnp.zeros_like(w_dst)

    barrier = pltpu.get_barrier_semaphore()
    greeted = (
        [at(y, x, p) for p in z_peers]
        + [at(y, p, z) for p in x_peers]
        + [at(p, x, z) for p in y_peers]
        + [{"ctx": c_next}, {"ctx": c_prev}, sibling, partner]
        + [{"ctx": c_next, **partner}, {"ctx": c_prev, **partner}]
    )
    for device in greeted:
        pl.semaphore_signal(barrier, inc=1, device_id=device, device_id_type=pl.DeviceIdType.MESH)

    loads = [
        pltpu.make_async_copy(q_hbm, q_buf, in_sem.at[0]),
        pltpu.make_async_copy(qr_hbm, qr_buf, in_sem.at[1]),
        pltpu.make_async_copy(o_hbm, o_buf, in_sem.at[2]),
    ]
    weights = [
        pltpu.make_async_copy(wk_hbm, wk_ref, in_sem.at[6]),
        pltpu.make_async_copy(wv_hbm, wv_ref, in_sem.at[7]),
    ]
    early = [
        pltpu.make_async_copy(len_hbm, len_ref, in_sem.at[8]),
        pltpu.make_async_copy(lat_hbm, lat_win.at[1], in_sem.at[3]),
        pltpu.make_async_copy(rope_hbm, rope_buf, in_sem.at[4]),
        pltpu.make_async_copy(pos_hbm, pos_ref, in_sem.at[5]),
    ]
    for copy in weights + early + loads:
        copy.start()
    for copy in weights:
        copy.wait()

    half = wk_ref.shape[1] // 2
    for q in range(4):
        rows = (wk_ref, wv_ref)[q // 2][...].astype(F32)
        pack[4 * q : 4 * q + 4, :] = rows[:, (q % 2) * half : (q % 2 + 1) * half]
    zbuf[z] = pack[...].astype(BF16)
    pl.semaphore_wait(barrier, len(greeted))

    def z_copy(d, slot):
        return remote(zbuf.at[slot], zbuf.at[slot], z_send.at[d], z_recv.at[d], at(y, x, z_peers[d]))

    for d in range(3):
        z_copy(d, z).start()

    for copy in early:
        copy.wait()
    rope = jnp.transpose(rope_buf[...].astype(F32))
    rot_win[1] = jnp.concatenate([rope, rope], axis=1).astype(BF16)

    blocks = [lax.rem(me + tokens + b - 1, tokens) for b in range(3)]
    index = lax.broadcasted_iota(jnp.int32, (1, len_ref.shape[1]), 1)
    lengths = len_ref[...]

    def frames(pos, block):
        start = jnp.sum(jnp.where(index <= block, lengths, 0), axis=1, keepdims=True)
        return block + (pos >= start).astype(jnp.int32)

    own = jnp.broadcast_to(pos_ref[pl.ds(me, 1), :], (TOK, TOK))
    own_pos = jnp.transpose(own)
    own_frame = frames(own_pos, me)
    for b in range(3):
        pos = jnp.broadcast_to(pos_ref[pl.ds(blocks[b], 1), :], (TOK, TOK))
        ok = (frames(pos, blocks[b]) <= own_frame) & (own_pos - pos < WINDOW)
        if b == 0:
            ok = ok & jnp.broadcast_to(me > 0, ok.shape)
        if b == 2:
            ok = ok & jnp.broadcast_to(me < tokens - 1, ok.shape)
        bias[:, b * TOK : (b + 1) * TOK] = jnp.where(ok, 0.0, MASKED)
    acc[...] = jnp.zeros_like(acc)

    for d in range(3):
        z_copy(d, z_peers[2 - d]).wait_recv()
    for s in range(NZ):
        piece = zbuf[s].astype(F32)
        for q in range(4):
            mix[q, 4 * s : 4 * s + 4, :] = piece[4 * q : 4 * q + 4, :]
    for j in range(CHUNKS):
        lanes = slice((j % 4) * WIDTH, (j % 4 + 1) * WIDTH)
        wk[j, y, x] = mix[j // 4, :, lanes].astype(BF16)
        wv[j, y, x] = mix[2 + j // 4, :, lanes].astype(BF16)

    up, down = at(y_up, x, z), at(y_down, x, z)
    left, right = at(y, x_down, z), at(y, x_up, z)

    def y_of(steps):
        return lax.rem(y + steps + NY, NY)

    def x_of(steps):
        return lax.rem(x + steps + NX, NX)

    def k_x(g, d, offset):
        part = wk.at[slice(*K_GROUPS[g]), y, x_of(offset)]
        n = 3 * g + d
        return remote(part, part, g_send.at[n], g_recv.at[n], at(y, x_peers[d], z))

    def v_direct(d, offset):
        part = wv.at[0:DIRECT, y_of(offset), x]
        n = 6 + d
        return remote(part, part, g_send.at[n], g_recv.at[n], at(y_peers[d], x, z))

    def v_hop(_, sign, depth, offset):
        part = wv.at[slice(*V_GROUP), y_of(offset), x]
        if depth == 3:
            part = part.at[:, :, : WIDTH // 2] if sign > 0 else part.at[:, :, WIDTH // 2 :]
        n = 13 + 2 * depth + (0 if sign > 0 else 1)
        return remote(part, part, g_send.at[n], g_recv.at[n], up if sign > 0 else down)

    def k_hop(j, sign, depth, offset):
        part = wk.at[j, y_of(offset)]
        if depth == 3:
            part = part.at[0:2] if sign > 0 else part.at[2:4]
        n = 2 * depth + (0 if sign > 0 else 1)
        return remote(part, part, c_send.at[j, n], c_recv.at[j, n], up if sign > 0 else down)

    def v_x(j, sign, depth, offset):
        part = wv.at[j, :, x_of(offset)]
        if depth == 1:
            part = wv.at[j, 0:4, x_of(offset)] if sign > 0 else wv.at[j, 4:8, x_of(offset)]
        n = 8 + 2 * depth + (0 if sign > 0 else 1)
        return remote(part, part, c_send.at[j, n], c_recv.at[j, n], right if sign > 0 else left)

    def arrive(make, j, sign, depth):
        make(j, sign, depth, -sign * (depth + 1)).wait_recv()

    def leave(make, j, sign, depth):
        return make(j, sign, depth, -sign * depth)

    def hop(make, j, n, last):
        for sign in (1, -1):
            if n > 0:
                arrive(make, j, sign, n - 1)
            if n < last:
                leave(make, j, sign, n).start()

    for d in range(NY - 1):
        v_direct(d, 0).start()
    for g in range(2):
        for d in range(3):
            k_x(g, d, 0).start()
        if g == 0:
            hop(v_hop, 0, 0, 4)

    halo = [
        remote(lat_win.at[1], lat_win.at[0], h_send.at[0], h_recv.at[0], {"ctx": c_next}),
        remote(lat_win.at[1], lat_win.at[2], h_send.at[1], h_recv.at[1], {"ctx": c_prev}),
        remote(rot_win.at[1], rot_win.at[0], h_send.at[2], h_recv.at[2], {"ctx": c_next}),
        remote(rot_win.at[1], rot_win.at[2], h_send.at[3], h_recv.at[3], {"ctx": c_prev}),
    ]
    for copy in halo:
        copy.start()

    def columns(j, width):
        return pl.ds(pl.multiple_of(j * width, width), width)

    def outs(i):
        plain, rot = columns(i, HEADS * DIM), columns(i, HEADS * ROPE)
        return [
            pltpu.make_async_copy(att_buf.at[:, plain], att_hbm.at[:, plain], out_sem.at[i, 0]),
            pltpu.make_async_copy(dq_buf.at[:, plain], dq_hbm.at[:, plain], out_sem.at[i, 1]),
            pltpu.make_async_copy(dqr_buf.at[:, rot], dqr_hbm.at[:, rot], out_sem.at[i, 2]),
        ]

    def both(ref, i):
        return jnp.concatenate([ref[2 * i + k].reshape(LATENT, WIDTH) for k in range(2)], axis=1)

    def compute(i):
        plain, rot_cols = columns(i, HEADS * DIM), columns(i, HEADS * ROPE)
        every = range(HEADS)
        cols = [slice(e * DIM, (e + 1) * DIM) for e in every]
        window = lat_win[...].reshape(3 * TOK, LATENT)
        rot = rot_win[...].reshape(3 * TOK, 2 * ROPE)
        key_w = both(wk, i)
        keys = dot(window, key_w, 1, 0).astype(BF16)
        queries, rots = q_buf[:, plain], qr_buf[:, rot_cols]
        first = lax.broadcasted_iota(jnp.int32, (TOK, 2 * ROPE), 1) < ROPE
        blank = jnp.zeros((TOK, 2 * ROPE), BF16)
        key, query = [], []
        for e in every:
            r_pair = rots[:, cols[e // 2]]
            r_own = jnp.where(first, r_pair, blank) if e % 2 == 0 else jnp.where(first, blank, r_pair)
            key.append(jnp.concatenate([keys[:, cols[e]], rot], axis=1))
            query.append(jnp.concatenate([queries[:, cols[e]], r_own], axis=1))
        scores = [dot(query[e], key[e], 1, 1) for e in every]
        value_w = both(wv, i)
        values = dot(window, value_w, 1, 0).astype(BF16)
        value = [values[:, cols[e]] for e in every]
        cots = o_buf[:, plain]
        cot = [cots[:, cols[e]] for e in every]
        mask = bias[...]
        weights = []
        for e in every:
            score = scores[e] * SCALE + mask
            top = jnp.max(score, axis=1, keepdims=True)
            weight = jnp.exp(score - top)
            weights.append(weight * (1.0 / jnp.sum(weight, axis=1, keepdims=True)))
        prob_grad = [dot(cot[e], value[e], 1, 1) for e in every]
        probs = [weight.astype(BF16) for weight in weights]
        out = [dot(probs[e], value[e], 1, 0).astype(BF16) for e in every]
        value_side = [dot(cot[e], probs[e], 0, 0).astype(BF16) for e in every]
        delta = [jnp.sum(cot[e].astype(F32) * out[e].astype(F32), axis=1, keepdims=True) for e in every]
        score_grad = [(weights[e] * (prob_grad[e] - delta[e])).astype(BF16) for e in every]
        key_side = [dot(query[e], score_grad[e], 0, 0) * SCALE for e in every]
        grad = [dot(score_grad[e], key[e], 1, 0) * SCALE for e in every]
        key_part = [side[:DIM].astype(BF16) for side in key_side]
        att_buf[:, plain] = jnp.concatenate(out, axis=1)
        dq_buf[:, plain] = jnp.concatenate([g[:, :DIM] for g in grad], axis=1)
        dqr_buf[:, rot_cols] = jnp.concatenate(
            [jnp.where(first, grad[e][:, DIM:], grad[e + 1][:, DIM:]) for e in range(0, HEADS, 2)], axis=1
        )
        back = dot(key_w, jnp.concatenate(key_part, axis=0), 1, 0)
        acc[:LATENT] += back + dot(value_w, jnp.concatenate(value_side, axis=0), 1, 0)
        acc[LATENT:] += sum(side[DIM:] for side in key_side[1:]) + key_side[0][DIM:]
        for copy in outs(i):
            copy.start()

    def slot(t, carry):
        def during(j, run):
            @pl.when((j >= 0) & (j < CHUNKS))
            def _():
                run(j)

        def once(when, run):
            @pl.when(t == when)
            def _():
                run()

        def k_arrive(g):
            for d in range(3):
                k_x(g, d, -(d + 1)).wait_recv()

        def v_arrive():
            for d in range(NY - 1):
                v_direct(d, -(d + 1)).wait_recv()

        for n in reversed(range(1, 5)):
            during(t - K_SLOTS[n], lambda j, n=n: hop(k_hop, j, n, 4))
        for n in reversed(range(1, 3)):
            during(t - V_SLOTS[n], lambda j, n=n: hop(v_x, j, n, 2))
        for g in range(2):
            once(K_GROUPS[g][0], lambda g=g: k_arrive(g))
        during(t - K_SLOTS[0], lambda j: hop(k_hop, j, 0, 4))
        once(V_SLOTS[0], v_arrive)
        for n in range(1, 5):
            once(V_HOPS[n - 1], lambda n=n: hop(v_hop, 0, n, 4))
        during(t - V_SLOTS[0], lambda j: hop(v_x, j, 0, 2))

        @pl.when(t == LAST + 1)
        def _():
            for copy in loads:
                copy.wait()
            for copy in halo:
                copy.wait_recv()

        @pl.when((t > LAST) & (lax.rem(t - LAST, 2) == 1))
        def _():
            compute(lax.div(t - LAST, 2))

        return carry

    lax.fori_loop(0, CHUNKS + LAST, slot, 0)

    acc[LATENT:ROWS] += acc[ROWS:]
    pieces = range(PIECES)

    def rows(owner, p):
        return pl.ds(pl.multiple_of(owner * HALF + p * PIECE, 16), PIECE)

    step1 = [remote(t1_src.at[p], t1_dst.at[p], t_send.at[p, 0], t_recv.at[p, 0], sibling) for p in pieces]
    step2 = [
        [
            remote(t2_src.at[p, k], t2_dst.at[p, k], t_send.at[p, 1 + k], t_recv.at[p, 1 + k], {"ctx": target})
            for k, target in enumerate((c_prev, c_next))
        ]
        for p in pieces
    ]
    far = [
        [
            [
                remote(t2_src.at[p, k], w_dst.at[p, n], w_send.at[p, n], w_recv.at[p, n], {"ctx": target, **half_of})
                for n, half_of in ((1, partner), (0, {}))
            ]
            for k, target in enumerate((c_prev, c_next))
        ]
        for p in pieces
    ]
    ends = (first_z, last_z)

    step3 = [remote(t3_src.at[p], t3_dst.at[p], t_send.at[p, 3], t_recv.at[p, 3], partner) for p in pieces]

    def step4(owner, p):
        return remote(t4.at[owner, p], t4.at[owner, p], t_send.at[p, 4], t_recv.at[p, 4], sibling)

    for p in pieces:
        t1_src[p] = acc[rows(1 - core, p)].astype(BF16)
        step1[p].start()
    centre = []
    for p in pieces:
        step1[p].wait_recv()
        mine = acc[rows(core, p)] + t1_dst[p].astype(F32)
        t2_src[p, 0] = mine[:, :TOK].astype(BF16)
        t2_src[p, 1] = mine[:, 2 * TOK :].astype(BF16)
        for k in range(2):
            pl.when(jnp.logical_not(ends[k]))(step2[p][k].start)

            @pl.when(ends[k])
            def _(p=p, k=k):
                for copy in far[p][k]:
                    copy.start()

        centre.append(mine[:, TOK : 2 * TOK])

    for d in range(3):
        z_copy(d, z).wait_send()
    for copy in halo:
        copy.wait_send()
    for d in range(NY - 1):
        v_direct(d, 0).wait_send()
    for g in range(2):
        for d in range(3):
            k_x(g, d, 0).wait_send()
    for sign in (1, -1):
        for depth in range(4):
            leave(v_hop, 0, sign, depth).wait_send()

    def drain(j, carry):
        for sign in (1, -1):
            for depth in range(4):
                leave(k_hop, j, sign, depth).wait_send()
            for depth in range(2):
                leave(v_x, j, sign, depth).wait_send()
        return carry

    lax.fori_loop(0, CHUNKS, drain, 0)

    def drain_outs(i, carry):
        for copy in outs(i):
            copy.wait()
        return carry

    lax.fori_loop(0, STEPS, drain_outs, 0)

    for p in pieces:
        for k in range(2):
            pl.when(jnp.logical_not(ends[1 - k]))(step2[p][k].wait_recv)
        t3_src[p] = (centre[p] + t2_dst[p, 0].astype(F32) + t2_dst[p, 1].astype(F32)).astype(BF16)
        step3[p].start()
    for p in pieces:
        step3[p].wait_recv()

        @pl.when(first_z | last_z)
        def _(p=p):
            for copy in far[p][0]:
                copy.wait_recv()

        near = t3_src[p].astype(F32) + t3_dst[p].astype(F32)
        t4[core, p] = near + (w_dst[p, 0].astype(F32) + w_dst[p, 1].astype(F32))
        step4(core, p).start()
    for p in pieces:
        step4(1 - core, p).wait_recv()
    whole = t4[...].reshape(ROWS, TOK)
    dlat_ref[...] = jnp.transpose(whole[:LATENT])
    drope_ref[...] = whole[LATENT:]
    for p in pieces:
        for copy in [step1[p], step3[p], step4(core, p)]:
            copy.wait_send()
        for k in range(2):
            pl.when(jnp.logical_not(ends[k]))(step2[p][k].wait_send)

            @pl.when(ends[k])
            def _(p=p, k=k):
                for copy in far[p][k]:
                    copy.wait_send()


PARTS = (2, 4, 2, 1, 1)


def write_out(*refs):
    count = len(PARTS)
    sources, targets, buffers = refs[:count], refs[count : 2 * count], refs[2 * count : 3 * count]
    came, left = refs[3 * count :]
    moves = []
    for source, target, buffer, parts in zip(sources, targets, buffers, PARTS):
        size = source.shape[0] // parts
        for p in range(parts):
            n = len(moves)
            rows = slice(p * size, (p + 1) * size)
            moves.append((
                pltpu.make_async_copy(source.at[rows], buffer.at[rows], came.at[n]),
                pltpu.make_async_copy(buffer.at[rows], target.at[rows], left.at[n]),
            ))
    for load, _ in moves:
        load.start()
    for load, store in moves:
        load.wait()
        store.start()
    for _, store in moves:
        store.wait()


def on_device(q_nope, q_rope, latent, key_rope, w_key, w_value, stripe, frame_len, out_grad):
    cols = q_nope.shape[1]
    rot_cols = q_rope.shape[1]
    positions = stripe.reshape(-1, TOK)
    lengths = frame_len.reshape(1, -1)
    vmem = pl.BlockSpec(memory_space=pltpu.VMEM)
    hbm = pl.BlockSpec(memory_space=pltpu.HBM)
    dma = pltpu.SemaphoreType.DMA
    outs = (
        jax.ShapeDtypeStruct((TOK, cols), BF16),
        jax.ShapeDtypeStruct((TOK, cols), F32),
        jax.ShapeDtypeStruct((TOK, rot_cols), F32),
        jax.ShapeDtypeStruct((TOK, LATENT), F32),
        jax.ShapeDtypeStruct((ROPE, TOK), F32),
    )
    results = pl.pallas_call(
        kernel,
        out_shape=outs,
        in_specs=[hbm] * 9,
        out_specs=(hbm, hbm, hbm, vmem, vmem),
        scratch_shapes=[
            pltpu.VMEM((TOK, cols), BF16),
            pltpu.VMEM((TOK, rot_cols), BF16),
            pltpu.VMEM((TOK, cols), BF16),
            pltpu.VMEM((ROPE, TOK), BF16),
            pltpu.VMEM(positions.shape, jnp.int32),
            pltpu.VMEM(w_key.shape, BF16),
            pltpu.VMEM(w_value.shape, BF16),
            pltpu.VMEM(lengths.shape, jnp.int32),
            pltpu.VMEM((TOK, cols), BF16),
            pltpu.VMEM((TOK, cols), F32),
            pltpu.VMEM((TOK, rot_cols), F32),
            pltpu.VMEM((16, cols // 2), F32),
            pltpu.VMEM((NZ, 16, cols // 2), BF16),
            pltpu.VMEM((4, 16, cols // 2), F32),
            pltpu.VMEM((CHUNKS, NY, NX, 16, WIDTH), BF16),
            pltpu.VMEM((CHUNKS, NY, NX, 16, WIDTH), BF16),
            pltpu.VMEM((3, TOK, LATENT), BF16),
            pltpu.VMEM((3, TOK, 2 * ROPE), BF16),
            pltpu.VMEM((TOK, 3 * TOK), F32),
            pltpu.VMEM((LATENT + 2 * ROPE, 3 * TOK), F32),
            pltpu.VMEM((PIECES, PIECE, 3 * TOK), BF16),
            pltpu.VMEM((PIECES, PIECE, 3 * TOK), BF16),
            pltpu.VMEM((PIECES, 2, PIECE, TOK), BF16),
            pltpu.VMEM((PIECES, 2, PIECE, TOK), BF16),
            pltpu.VMEM((PIECES, 2, PIECE, TOK), BF16),
            pltpu.VMEM((PIECES, PIECE, TOK), BF16),
            pltpu.VMEM((PIECES, PIECE, TOK), BF16),
            pltpu.VMEM((2, PIECES, PIECE, TOK), F32),
            dma((9,)),
            dma((STEPS, 3)),
            dma((3,)),
            dma((3,)),
            dma((4,)),
            dma((4,)),
            dma((21,)),
            dma((21,)),
            dma((CHUNKS, 12)),
            dma((CHUNKS, 12)),
            dma((PIECES, 5)),
            dma((PIECES, 5)),
            dma((PIECES, 2)),
            dma((PIECES, 2)),
        ],
        compiler_params=pltpu.CompilerParams(
            collective_id=0, has_side_effects=True, vmem_limit_bytes=VMEM_BYTES
        ),
        cost_estimate=pl.CostEstimate(flops=4_700_000_000, bytes_accessed=5_000_000, transcendentals=800_000),
        name="latent_attention",
    )(q_nope, q_rope, latent, key_rope.T, w_key, w_value, positions, lengths, out_grad)
    attended, dq_nope, dq_rope, d_latent, d_key_rope = pl.pallas_call(
        write_out,
        out_shape=outs,
        in_specs=[hbm] * len(outs),
        out_specs=(hbm,) * len(outs),
        compiler_params=pltpu.CompilerParams(vmem_limit_bytes=VMEM_BYTES),
        scratch_shapes=[pltpu.VMEM(out.shape, out.dtype) for out in outs] + [dma((sum(PARTS),))] * 2,
        name="write_out",
    )(*results)
    return attended, dq_nope, dq_rope, d_latent, d_key_rope.T


def solution(mesh):
    return jax.shard_map(
        on_device,
        mesh=mesh,
        in_specs=(
            P("ctx", "head"),
            P("ctx", "head"),
            P("ctx", None),
            P("ctx", None),
            P("ctx", "head"),
            P("ctx", "head"),
            P(),
            P(),
            P("ctx", "head"),
        ),
        out_specs=(
            P("ctx", "head"),
            P("ctx", "head"),
            P("ctx", "head"),
            P("ctx", None),
            P("ctx", None),
        ),
        check_vma=False,
    )
```

```python
import jax
import jax.numpy as jnp
from jax import lax
from jax.experimental import pallas as pl
from jax.experimental.pallas import tpu as pltpu
from jax.sharding import PartitionSpec as P

HEAD_QK = 192
WINDOW = 128
SCALE = HEAD_QK ** (-0.5)
MASKED = -1e30
VMEM_BYTES = 60 * 1024 * 1024

NY, NX, NZ = 8, 4, 4
TOK = 128
LATENT = 512
ROPE = 64
DIM = 128
CHUNKS = 8
WIDTH = 2 * DIM
STEPS = CHUNKS // 2
HEADS = 4
PIECES = 2
ROWS = LATENT + ROPE
HALF = ROWS // 2
PIECE = HALF // PIECES
K_SLOTS = (0, 3, 5, 7, 9)
V_SLOTS = (3, 6, 8)
K_GROUPS = ((0, 2), (2, CHUNKS))
DIRECT = 3
V_GROUP = (DIRECT, CHUNKS)
V_HOPS = (1, 3, 5, 6)
LAST = max(K_SLOTS[-1], V_SLOTS[-1])

BF16 = jnp.bfloat16
F32 = jnp.float32


def dot(a, b, ca, cb):
    return lax.dot_general(a, b, (((ca,), (cb,)), ((), ())), preferred_element_type=F32)


def kernel(
    q_hbm, qr_hbm, lat_hbm, rope_hbm, wk_hbm, wv_hbm, pos_hbm, len_hbm, o_hbm,
    att_hbm, dq_hbm, dqr_hbm, dlat_ref, drope_ref,
    q_buf, qr_buf, o_buf, rope_buf, pos_ref, wk_ref, wv_ref, len_ref, att_buf, dq_buf, dqr_buf,
    pack, zbuf, mix, wk, wv, lat_win, rot_win, bias, acc,
    t1_src, t1_dst, t2_src, t2_dst, w_dst, t3_src, t3_dst, t4,
    in_sem, out_sem, z_send, z_recv, h_send, h_recv, g_send, g_recv, c_send, c_recv, t_send, t_recv, w_send, w_recv,
):
    me = lax.axis_index("ctx")
    head = lax.axis_index("head")
    z = lax.rem(me, NZ)
    x = lax.rem(lax.div(me, NZ), NX)
    y = lax.div(me, NZ * NX)
    core = lax.rem(head, 2)
    z_hi = lax.div(head, 2)

    def at(y_, x_, z_):
        return {"ctx": (y_ * NX + x_) * NZ + z_}

    z_peers = [lax.rem(z + d, NZ) for d in (1, 2, 3)]
    x_peers = [lax.rem(x + d, NX) for d in (1, 2, 3)]
    y_peers = [lax.rem(y + d, NY) for d in range(1, NY)]
    y_up, y_down = y_peers[0], y_peers[-1]
    x_up, x_down = x_peers[0], x_peers[2]
    tokens = NY * NX * NZ
    c_next, c_prev = lax.rem(me + 1, tokens), lax.rem(me + tokens - 1, tokens)
    sibling = {"head": z_hi * 2 + (1 - core)}
    partner = {"head": (1 - z_hi) * 2 + core}
    first_z, last_z = z == 0, z == NZ - 1

    def remote(src, dst, send, recv, device):
        return pltpu.make_async_remote_copy(
            src_ref=src, dst_ref=dst, send_sem=send, recv_sem=recv,
            device_id=device, device_id_type=pl.DeviceIdType.MESH,
        )

    t2_dst[...] = jnp.zeros_like(t2_dst)
    w_dst[...] = jnp.zeros_like(w_dst)

    barrier = pltpu.get_barrier_semaphore()
    greeted = (
        [at(y, x, p) for p in z_peers]
        + [at(y, p, z) for p in x_peers]
        + [at(p, x, z) for p in y_peers]
        + [{"ctx": c_next}, {"ctx": c_prev}, sibling, partner]
        + [{"ctx": c_next, **partner}, {"ctx": c_prev, **partner}]
    )
    for device in greeted:
        pl.semaphore_signal(barrier, inc=1, device_id=device, device_id_type=pl.DeviceIdType.MESH)

    loads = [
        pltpu.make_async_copy(q_hbm, q_buf, in_sem.at[0]),
        pltpu.make_async_copy(qr_hbm, qr_buf, in_sem.at[1]),
        pltpu.make_async_copy(o_hbm, o_buf, in_sem.at[2]),
    ]
    weights = [
        pltpu.make_async_copy(wk_hbm, wk_ref, in_sem.at[6]),
        pltpu.make_async_copy(wv_hbm, wv_ref, in_sem.at[7]),
    ]
    early = [
        pltpu.make_async_copy(len_hbm, len_ref, in_sem.at[8]),
        pltpu.make_async_copy(lat_hbm, lat_win.at[1], in_sem.at[3]),
        pltpu.make_async_copy(rope_hbm, rope_buf, in_sem.at[4]),
        pltpu.make_async_copy(pos_hbm, pos_ref, in_sem.at[5]),
    ]
    for copy in weights + early + loads:
        copy.start()
    for copy in weights:
        copy.wait()

    half = wk_ref.shape[1] // 2
    for q in range(4):
        rows = (wk_ref, wv_ref)[q // 2][...].astype(F32)
        pack[4 * q : 4 * q + 4, :] = rows[:, (q % 2) * half : (q % 2 + 1) * half]
    zbuf[z] = pack[...].astype(BF16)
    pl.semaphore_wait(barrier, len(greeted))

    def z_copy(d, slot):
        return remote(zbuf.at[slot], zbuf.at[slot], z_send.at[d], z_recv.at[d], at(y, x, z_peers[d]))

    for d in range(3):
        z_copy(d, z).start()

    for copy in early:
        copy.wait()
    rope = jnp.transpose(rope_buf[...].astype(F32))
    rot_win[1] = jnp.concatenate([rope, rope], axis=1).astype(BF16)

    blocks = [lax.rem(me + tokens + b - 1, tokens) for b in range(3)]
    index = lax.broadcasted_iota(jnp.int32, (1, len_ref.shape[1]), 1)
    lengths = len_ref[...]

    def frames(pos, block):
        start = jnp.sum(jnp.where(index <= block, lengths, 0), axis=1, keepdims=True)
        return block + (pos >= start).astype(jnp.int32)

    own = jnp.broadcast_to(pos_ref[pl.ds(me, 1), :], (TOK, TOK))
    own_pos = jnp.transpose(own)
    own_frame = frames(own_pos, me)
    for b in range(3):
        pos = jnp.broadcast_to(pos_ref[pl.ds(blocks[b], 1), :], (TOK, TOK))
        ok = (frames(pos, blocks[b]) <= own_frame) & (own_pos - pos < WINDOW)
        if b == 0:
            ok = ok & jnp.broadcast_to(me > 0, ok.shape)
        if b == 2:
            ok = ok & jnp.broadcast_to(me < tokens - 1, ok.shape)
        bias[:, b * TOK : (b + 1) * TOK] = jnp.where(ok, 0.0, MASKED)
    acc[...] = jnp.zeros_like(acc)

    for d in range(3):
        z_copy(d, z_peers[2 - d]).wait_recv()
    for s in range(NZ):
        piece = zbuf[s].astype(F32)
        for q in range(4):
            mix[q, 4 * s : 4 * s + 4, :] = piece[4 * q : 4 * q + 4, :]
    def assemble(target, first, chunks):
        for j in chunks:
            lanes = slice((j % 4) * WIDTH, (j % 4 + 1) * WIDTH)
            target[j, y, x] = mix[first + j // 4, :, lanes].astype(BF16)

    up, down = at(y_up, x, z), at(y_down, x, z)
    left, right = at(y, x_down, z), at(y, x_up, z)

    def y_of(steps):
        return lax.rem(y + steps + NY, NY)

    def x_of(steps):
        return lax.rem(x + steps + NX, NX)

    def k_x(g, d, offset):
        part = wk.at[slice(*K_GROUPS[g]), y, x_of(offset)]
        n = 3 * g + d
        return remote(part, part, g_send.at[n], g_recv.at[n], at(y, x_peers[d], z))

    def v_direct(d, offset):
        part = wv.at[0:DIRECT, y_of(offset), x]
        n = 6 + d
        return remote(part, part, g_send.at[n], g_recv.at[n], at(y_peers[d], x, z))

    def v_hop(_, sign, depth, offset):
        part = wv.at[slice(*V_GROUP), y_of(offset), x]
        if depth == 3:
            part = part.at[:, :, : WIDTH // 2] if sign > 0 else part.at[:, :, WIDTH // 2 :]
        n = 13 + 2 * depth + (0 if sign > 0 else 1)
        return remote(part, part, g_send.at[n], g_recv.at[n], up if sign > 0 else down)

    def k_hop(j, sign, depth, offset):
        part = wk.at[j, y_of(offset)]
        if depth == 3:
            part = part.at[0:2] if sign > 0 else part.at[2:4]
        n = 2 * depth + (0 if sign > 0 else 1)
        return remote(part, part, c_send.at[j, n], c_recv.at[j, n], up if sign > 0 else down)

    def v_x(j, sign, depth, offset):
        part = wv.at[j, :, x_of(offset)]
        if depth == 1:
            part = wv.at[j, 0:4, x_of(offset)] if sign > 0 else wv.at[j, 4:8, x_of(offset)]
        n = 8 + 2 * depth + (0 if sign > 0 else 1)
        return remote(part, part, c_send.at[j, n], c_recv.at[j, n], right if sign > 0 else left)

    def arrive(make, j, sign, depth):
        make(j, sign, depth, -sign * (depth + 1)).wait_recv()

    def leave(make, j, sign, depth):
        return make(j, sign, depth, -sign * depth)

    def hop(make, j, n, last):
        for sign in (1, -1):
            if n > 0:
                arrive(make, j, sign, n - 1)
            if n < last:
                leave(make, j, sign, n).start()

    assemble(wv, 2, range(DIRECT))
    for d in range(NY - 1):
        v_direct(d, 0).start()
    for g in range(2):
        assemble(wk, 0, range(*K_GROUPS[g]))
        for d in range(3):
            k_x(g, d, 0).start()
        if g == 0:
            assemble(wv, 2, range(*V_GROUP))
            hop(v_hop, 0, 0, 4)

    halo = [
        remote(lat_win.at[1], lat_win.at[0], h_send.at[0], h_recv.at[0], {"ctx": c_next}),
        remote(lat_win.at[1], lat_win.at[2], h_send.at[1], h_recv.at[1], {"ctx": c_prev}),
        remote(rot_win.at[1], rot_win.at[0], h_send.at[2], h_recv.at[2], {"ctx": c_next}),
        remote(rot_win.at[1], rot_win.at[2], h_send.at[3], h_recv.at[3], {"ctx": c_prev}),
    ]
    for copy in halo:
        copy.start()

    def columns(j, width):
        return pl.ds(pl.multiple_of(j * width, width), width)

    def outs(i):
        plain, rot = columns(i, HEADS * DIM), columns(i, HEADS * ROPE)
        return [
            pltpu.make_async_copy(att_buf.at[:, plain], att_hbm.at[:, plain], out_sem.at[i, 0]),
            pltpu.make_async_copy(dq_buf.at[:, plain], dq_hbm.at[:, plain], out_sem.at[i, 1]),
            pltpu.make_async_copy(dqr_buf.at[:, rot], dqr_hbm.at[:, rot], out_sem.at[i, 2]),
        ]

    def both(ref, i):
        return jnp.concatenate([ref[2 * i + k].reshape(LATENT, WIDTH) for k in range(2)], axis=1)

    def compute(i):
        plain, rot_cols = columns(i, HEADS * DIM), columns(i, HEADS * ROPE)
        every = range(HEADS)
        cols = [slice(e * DIM, (e + 1) * DIM) for e in every]
        window = lat_win[...].reshape(3 * TOK, LATENT)
        rot = rot_win[...].reshape(3 * TOK, 2 * ROPE)
        key_w = both(wk, i)
        keys = dot(window, key_w, 1, 0).astype(BF16)
        queries, rots = q_buf[:, plain], qr_buf[:, rot_cols]
        first = lax.broadcasted_iota(jnp.int32, (TOK, 2 * ROPE), 1) < ROPE
        blank = jnp.zeros((TOK, 2 * ROPE), BF16)
        key, query = [], []
        for e in every:
            r_pair = rots[:, cols[e // 2]]
            r_own = jnp.where(first, r_pair, blank) if e % 2 == 0 else jnp.where(first, blank, r_pair)
            key.append(jnp.concatenate([keys[:, cols[e]], rot], axis=1))
            query.append(jnp.concatenate([queries[:, cols[e]], r_own], axis=1))
        scores = [dot(query[e], key[e], 1, 1) for e in every]
        value_w = both(wv, i)
        values = dot(window, value_w, 1, 0).astype(BF16)
        value = [values[:, cols[e]] for e in every]
        cots = o_buf[:, plain]
        cot = [cots[:, cols[e]] for e in every]
        mask = bias[...]
        weights = []
        for e in every:
            score = scores[e] * SCALE + mask
            top = jnp.max(score, axis=1, keepdims=True)
            weight = jnp.exp(score - top)
            weights.append(weight * (1.0 / jnp.sum(weight, axis=1, keepdims=True)))
        prob_grad = [dot(cot[e], value[e], 1, 1) for e in every]
        probs = [weight.astype(BF16) for weight in weights]
        out = [dot(probs[e], value[e], 1, 0).astype(BF16) for e in every]
        value_side = [dot(cot[e], probs[e], 0, 0).astype(BF16) for e in every]
        delta = [jnp.sum(cot[e].astype(F32) * out[e].astype(F32), axis=1, keepdims=True) for e in every]
        score_grad = [(weights[e] * (prob_grad[e] - delta[e])).astype(BF16) for e in every]
        key_side = [dot(query[e], score_grad[e], 0, 0) * SCALE for e in every]
        grad = [dot(score_grad[e], key[e], 1, 0) * SCALE for e in every]
        key_part = [side[:DIM].astype(BF16) for side in key_side]
        att_buf[:, plain] = jnp.concatenate(out, axis=1)
        dq_buf[:, plain] = jnp.concatenate([g[:, :DIM] for g in grad], axis=1)
        dqr_buf[:, rot_cols] = jnp.concatenate(
            [jnp.where(first, grad[e][:, DIM:], grad[e + 1][:, DIM:]) for e in range(0, HEADS, 2)], axis=1
        )
        back = dot(key_w, jnp.concatenate(key_part, axis=0), 1, 0)
        acc[:LATENT] += back + dot(value_w, jnp.concatenate(value_side, axis=0), 1, 0)
        acc[LATENT:] += sum(side[DIM:] for side in key_side[1:]) + key_side[0][DIM:]
        for copy in outs(i):
            copy.start()

    def slot(t, carry):
        def during(j, run):
            @pl.when((j >= 0) & (j < CHUNKS))
            def _():
                run(j)

        def once(when, run):
            @pl.when(t == when)
            def _():
                run()

        def k_arrive(g):
            for d in range(3):
                k_x(g, d, -(d + 1)).wait_recv()

        def v_arrive():
            for d in range(NY - 1):
                v_direct(d, -(d + 1)).wait_recv()

        for n in reversed(range(1, 5)):
            during(t - K_SLOTS[n], lambda j, n=n: hop(k_hop, j, n, 4))
        for n in reversed(range(1, 3)):
            during(t - V_SLOTS[n], lambda j, n=n: hop(v_x, j, n, 2))
        for g in range(2):
            once(K_GROUPS[g][0], lambda g=g: k_arrive(g))
        during(t - K_SLOTS[0], lambda j: hop(k_hop, j, 0, 4))
        once(V_SLOTS[0], v_arrive)
        for n in range(1, 5):
            once(V_HOPS[n - 1], lambda n=n: hop(v_hop, 0, n, 4))
        during(t - V_SLOTS[0], lambda j: hop(v_x, j, 0, 2))

        @pl.when(t == LAST + 1)
        def _():
            for copy in loads:
                copy.wait()
            for copy in halo:
                copy.wait_recv()

        @pl.when((t > LAST) & (lax.rem(t - LAST, 2) == 1))
        def _():
            compute(lax.div(t - LAST, 2))

        return carry

    lax.fori_loop(0, CHUNKS + LAST, slot, 0)

    acc[LATENT:ROWS] += acc[ROWS:]
    pieces = range(PIECES)

    def rows(owner, p):
        return pl.ds(pl.multiple_of(owner * HALF + p * PIECE, 16), PIECE)

    step1 = [remote(t1_src.at[p], t1_dst.at[p], t_send.at[p, 0], t_recv.at[p, 0], sibling) for p in pieces]
    step2 = [
        [
            remote(t2_src.at[p, k], t2_dst.at[p, k], t_send.at[p, 1 + k], t_recv.at[p, 1 + k], {"ctx": target})
            for k, target in enumerate((c_prev, c_next))
        ]
        for p in pieces
    ]
    far = [
        [
            [
                remote(t2_src.at[p, k], w_dst.at[p, n], w_send.at[p, n], w_recv.at[p, n], {"ctx": target, **half_of})
                for n, half_of in ((1, partner), (0, {}))
            ]
            for k, target in enumerate((c_prev, c_next))
        ]
        for p in pieces
    ]
    ends = (first_z, last_z)

    step3 = [remote(t3_src.at[p], t3_dst.at[p], t_send.at[p, 3], t_recv.at[p, 3], partner) for p in pieces]

    def step4(owner, p):
        return remote(t4.at[owner, p], t4.at[owner, p], t_send.at[p, 4], t_recv.at[p, 4], sibling)

    for p in pieces:
        t1_src[p] = acc[rows(1 - core, p)].astype(BF16)
        step1[p].start()
    centre = []
    for p in pieces:
        step1[p].wait_recv()
        mine = acc[rows(core, p)] + t1_dst[p].astype(F32)
        t2_src[p, 0] = mine[:, :TOK].astype(BF16)
        t2_src[p, 1] = mine[:, 2 * TOK :].astype(BF16)
        for k in range(2):
            pl.when(jnp.logical_not(ends[k]))(step2[p][k].start)

            @pl.when(ends[k])
            def _(p=p, k=k):
                for copy in far[p][k]:
                    copy.start()

        centre.append(mine[:, TOK : 2 * TOK])

    for d in range(3):
        z_copy(d, z).wait_send()
    for copy in halo:
        copy.wait_send()
    for d in range(NY - 1):
        v_direct(d, 0).wait_send()
    for g in range(2):
        for d in range(3):
            k_x(g, d, 0).wait_send()
    for sign in (1, -1):
        for depth in range(4):
            leave(v_hop, 0, sign, depth).wait_send()

    def drain(j, carry):
        for sign in (1, -1):
            for depth in range(4):
                leave(k_hop, j, sign, depth).wait_send()
            for depth in range(2):
                leave(v_x, j, sign, depth).wait_send()
        return carry

    lax.fori_loop(0, CHUNKS, drain, 0)

    def drain_outs(i, carry):
        for copy in outs(i):
            copy.wait()
        return carry

    lax.fori_loop(0, STEPS, drain_outs, 0)

    for p in pieces:
        for k in range(2):
            pl.when(jnp.logical_not(ends[1 - k]))(step2[p][k].wait_recv)
        t3_src[p] = (centre[p] + t2_dst[p, 0].astype(F32) + t2_dst[p, 1].astype(F32)).astype(BF16)
        step3[p].start()
    for p in pieces:
        step3[p].wait_recv()

        @pl.when(first_z | last_z)
        def _(p=p):
            for copy in far[p][0]:
                copy.wait_recv()

        near = t3_src[p].astype(F32) + t3_dst[p].astype(F32)
        t4[core, p] = near + (w_dst[p, 0].astype(F32) + w_dst[p, 1].astype(F32))
        step4(core, p).start()
    for p in pieces:
        step4(1 - core, p).wait_recv()
    whole = t4[...].reshape(ROWS, TOK)
    dlat_ref[...] = jnp.transpose(whole[:LATENT])
    drope_ref[...] = whole[LATENT:]
    for p in pieces:
        for copy in [step1[p], step3[p], step4(core, p)]:
            copy.wait_send()
        for k in range(2):
            pl.when(jnp.logical_not(ends[k]))(step2[p][k].wait_send)

            @pl.when(ends[k])
            def _(p=p, k=k):
                for copy in far[p][k]:
                    copy.wait_send()


PARTS = (2, 4, 2, 1, 1)


def write_out(*refs):
    count = len(PARTS)
    sources, targets, buffers = refs[:count], refs[count : 2 * count], refs[2 * count : 3 * count]
    came, left = refs[3 * count :]
    moves = []
    for source, target, buffer, parts in zip(sources, targets, buffers, PARTS):
        size = source.shape[0] // parts
        for p in range(parts):
            n = len(moves)
            rows = slice(p * size, (p + 1) * size)
            moves.append((
                pltpu.make_async_copy(source.at[rows], buffer.at[rows], came.at[n]),
                pltpu.make_async_copy(buffer.at[rows], target.at[rows], left.at[n]),
            ))
    for load, _ in moves:
        load.start()
    for load, store in moves:
        load.wait()
        store.start()
    for _, store in moves:
        store.wait()


def on_device(q_nope, q_rope, latent, key_rope, w_key, w_value, stripe, frame_len, out_grad):
    cols = q_nope.shape[1]
    rot_cols = q_rope.shape[1]
    positions = stripe.reshape(-1, TOK)
    lengths = frame_len.reshape(1, -1)
    vmem = pl.BlockSpec(memory_space=pltpu.VMEM)
    hbm = pl.BlockSpec(memory_space=pltpu.HBM)
    dma = pltpu.SemaphoreType.DMA
    outs = (
        jax.ShapeDtypeStruct((TOK, cols), BF16),
        jax.ShapeDtypeStruct((TOK, cols), F32),
        jax.ShapeDtypeStruct((TOK, rot_cols), F32),
        jax.ShapeDtypeStruct((TOK, LATENT), F32),
        jax.ShapeDtypeStruct((ROPE, TOK), F32),
    )
    results = pl.pallas_call(
        kernel,
        out_shape=outs,
        in_specs=[hbm] * 9,
        out_specs=(hbm, hbm, hbm, vmem, vmem),
        scratch_shapes=[
            pltpu.VMEM((TOK, cols), BF16),
            pltpu.VMEM((TOK, rot_cols), BF16),
            pltpu.VMEM((TOK, cols), BF16),
            pltpu.VMEM((ROPE, TOK), BF16),
            pltpu.VMEM(positions.shape, jnp.int32),
            pltpu.VMEM(w_key.shape, BF16),
            pltpu.VMEM(w_value.shape, BF16),
            pltpu.VMEM(lengths.shape, jnp.int32),
            pltpu.VMEM((TOK, cols), BF16),
            pltpu.VMEM((TOK, cols), F32),
            pltpu.VMEM((TOK, rot_cols), F32),
            pltpu.VMEM((16, cols // 2), F32),
            pltpu.VMEM((NZ, 16, cols // 2), BF16),
            pltpu.VMEM((4, 16, cols // 2), F32),
            pltpu.VMEM((CHUNKS, NY, NX, 16, WIDTH), BF16),
            pltpu.VMEM((CHUNKS, NY, NX, 16, WIDTH), BF16),
            pltpu.VMEM((3, TOK, LATENT), BF16),
            pltpu.VMEM((3, TOK, 2 * ROPE), BF16),
            pltpu.VMEM((TOK, 3 * TOK), F32),
            pltpu.VMEM((LATENT + 2 * ROPE, 3 * TOK), F32),
            pltpu.VMEM((PIECES, PIECE, 3 * TOK), BF16),
            pltpu.VMEM((PIECES, PIECE, 3 * TOK), BF16),
            pltpu.VMEM((PIECES, 2, PIECE, TOK), BF16),
            pltpu.VMEM((PIECES, 2, PIECE, TOK), BF16),
            pltpu.VMEM((PIECES, 2, PIECE, TOK), BF16),
            pltpu.VMEM((PIECES, PIECE, TOK), BF16),
            pltpu.VMEM((PIECES, PIECE, TOK), BF16),
            pltpu.VMEM((2, PIECES, PIECE, TOK), F32),
            dma((9,)),
            dma((STEPS, 3)),
            dma((3,)),
            dma((3,)),
            dma((4,)),
            dma((4,)),
            dma((21,)),
            dma((21,)),
            dma((CHUNKS, 12)),
            dma((CHUNKS, 12)),
            dma((PIECES, 5)),
            dma((PIECES, 5)),
            dma((PIECES, 2)),
            dma((PIECES, 2)),
        ],
        compiler_params=pltpu.CompilerParams(
            collective_id=0, has_side_effects=True, vmem_limit_bytes=VMEM_BYTES
        ),
        cost_estimate=pl.CostEstimate(flops=4_700_000_000, bytes_accessed=5_000_000, transcendentals=800_000),
        name="latent_attention",
    )(q_nope, q_rope, latent, key_rope.T, w_key, w_value, positions, lengths, out_grad)
    attended, dq_nope, dq_rope, d_latent, d_key_rope = pl.pallas_call(
        write_out,
        out_shape=outs,
        in_specs=[hbm] * len(outs),
        out_specs=(hbm,) * len(outs),
        compiler_params=pltpu.CompilerParams(vmem_limit_bytes=VMEM_BYTES),
        scratch_shapes=[pltpu.VMEM(out.shape, out.dtype) for out in outs] + [dma((sum(PARTS),))] * 2,
        name="write_out",
    )(*results)
    return attended, dq_nope, dq_rope, d_latent, d_key_rope.T


def solution(mesh):
    return jax.shard_map(
        on_device,
        mesh=mesh,
        in_specs=(
            P("ctx", "head"),
            P("ctx", "head"),
            P("ctx", None),
            P("ctx", None),
            P("ctx", "head"),
            P("ctx", "head"),
            P(),
            P(),
            P("ctx", "head"),
        ),
        out_specs=(
            P("ctx", "head"),
            P("ctx", "head"),
            P("ctx", "head"),
            P("ctx", None),
            P("ctx", None),
        ),
        check_vma=False,
    )
```
